512 devices in a mesh: dp: 32 (over z, x_hi), tensor: 16 (over y, x_lo, core).
Axes of the slice: x: 4 (x_hi: 2, x_lo: 2; x = x_hi * 2 + x_lo), y: 4, z: 16, core: 2. Of those that a mesh axis runs over, the one named last changes fastest.
Arguments:
- hidden: bfloat16 [4096, 4096], P(('dp', 'tensor')), parts along dimension 0, may hold values from -6 to 6
- in_weight: bfloat16 [4096, 6208], P('tensor'), may hold values from -0.09375 to 0.09375
- out_weight: bfloat16 [2048, 4096], P(None, 'tensor'), may hold values from -0.125 to 0.125
- conv_weight: float32 [4, 4096], replicated, may hold values from -3 to 3
- head_params: float32 [3, 64], replicated, may hold values from -5.3 to 1.5, as said below
- packing: int32 [5], replicated, may hold values from 0 to 4, each once
- head_group: int32 [64], replicated, may hold values from 0 to 7, as said below
Outputs:
- layer_out: bfloat16 [4096, 4096], P(('dp', 'tensor')), parts along dimension 0
The draws below stay inside these ranges and needn't reach their ends.
There are 32 independent parts, one for each index of `dp`. The reference program is written for one: setup_inputs(seed, part) draws one part's arguments, and reference() takes and returns one part's arrays. A program takes and returns all parts, laid end to end along the dimension named above; an argument that names none is the same for every part. Nothing has to cross between parts.
Inputs may be any that keep to these rules, and one draw needn't show every extreme that they name: `packing`: each segment is named once. `head_group`: each group holds exactly 8 heads. `head_params`: row 0 lies in -4 to -1, row 1 holds logarithms of decay rates, row 2 lies in 0.5 to 1.5.
All inputs are finite; a program needn't handle non-finite values.
Results may differ from the reference program's by a relative error of at most 0.023.
Values may be sent and summed in bfloat16 or wider, within the bound.
No kernel may reach another device: no remote copies, remote signals or barrier semaphores. Data moves between devices by JAX's collectives and lax.ppermute only.
A program may use at most 64 MiB of HBM per device.

```python
import math
import jax
import jax.numpy as jnp
from jax import lax

D = 4096
HEADS = 64
HEAD_DIM = 32
GROUPS = 8
STATE = 128
CONV_K = 4
SEQ = 128
INNER = 2048
COLS = 6208


def draw_head_params(key, part):
    key = jax.random.fold_in(key, 7)
    keys = jax.random.split(key, 3)
    shifts = jax.random.uniform(keys[0], (HEADS,), jnp.float32, -4.0, -1.0)
    rate_log = jax.random.uniform(keys[1], (HEADS,), jnp.float32, math.log(0.02), math.log(4.0))
    skips = jax.random.uniform(keys[2], (HEADS,), jnp.float32, 0.5, 1.5)
    return jnp.stack([shifts, rate_log, skips])


def draw_head_group(key, part):
    key = jax.random.fold_in(key, 11)
    return (jax.random.permutation(key, HEADS) // (HEADS // GROUPS)).astype(jnp.int32)


def block_levels(stream_key, shape, shards, smallest, top_value):
    level, own = 1.0, jax.random.fold_in(stream_key, 6)
    for dim, shards_of in shards:
        heights = jnp.exp(jax.random.uniform(jax.random.fold_in(own, dim), (shards_of,), jnp.float32, smallest / len(shards), top_value / len(shards)))
        level = level * jnp.repeat(heights, shape[dim] // shards_of).reshape([-1 if axis == dim else 1 for axis in range(len(shape))])
    return level


def centred(key, dims, deviation, limit, shards=(), held_as=jnp.bfloat16):
    values = deviation * jax.random.normal(key, dims, jnp.float32)
    if shards:
        values = values * block_levels(key, dims, shards, -0.22, 0.18)
    return jnp.clip(values, -limit, limit).astype(held_as)


def setup_inputs(seed: int = 0, part: int = 0) -> dict:
    seeds = jax.random.split(jax.random.key(seed), 8)
    own_keys = jax.random.split(jax.random.fold_in(seeds[7], part), 8)
    return {
        "hidden": centred(own_keys[0], (SEQ, D), 1.0, 6.0, ((0, 16),)),
        "in_weight": centred(seeds[1], (D, COLS), D ** -0.5, 0.09375, ((0, 16),)),
        "out_weight": centred(seeds[2], (INNER, D), INNER ** -0.5, 0.125, ((1, 16),)),
        "conv_weight": centred(seeds[3], (CONV_K, INNER + 2 * GROUPS * STATE), 0.5, 3.0, (), jnp.float32),
        "head_params": draw_head_params(jax.random.fold_in(seeds[7], 71), part),
        "packing": jax.random.permutation(seeds[5], 5).astype(jnp.int32),
        "head_group": draw_head_group(jax.random.fold_in(seeds[7], 71), part),
    }


epsilon = 1e-05

def segment_offsets(packing, widths):
    width_table = jnp.array(widths, dtype=jnp.int32)
    placed = jnp.take(width_table, packing)
    starts = (jnp.cumsum(placed) - placed).astype(jnp.int32)
    return [jnp.sum(jnp.where(packing == number, starts, 0)).astype(jnp.int32) for number in range(5)]

def causal_conv(values, conv_taps):
    length = values.shape[0]
    kernel = conv_taps.shape[0]
    padded = jnp.pad(values.astype(jnp.float32), ((kernel - 1, 0), (0, 0)))
    summed = jnp.zeros(values.shape, jnp.float32)
    for offset in range(kernel):
        summed = summed + conv_taps[offset] * padded[offset:offset + length]
    return jax.nn.silu(summed).astype(jnp.bfloat16)

def state_mixing(x_heads, b_heads, c_heads, step_size, cumulative):
    length = x_heads.shape[0]
    scores = jnp.einsum('thn,shn->hts', c_heads, b_heads, precision=lax.Precision.HIGHEST)
    positions = jnp.arange(length)
    causal = positions[:, None] >= positions[None, :]
    spread = cumulative.T[:, :, None] - cumulative.T[:, None, :]
    weights = jnp.where(causal[None], jnp.exp(jnp.where(causal[None], spread, 0.0)), 0.0)
    weights = weights * scores * step_size.T[:, None, :]
    return jnp.einsum('hts,shp->thp', weights, x_heads, precision=lax.Precision.HIGHEST)

def gated_heads(gate_raw, x_values, b_full, c_full, dt_raw, params, member):
    length = x_values.shape[0]
    head_count = member.shape[0]
    x_heads = x_values.astype(jnp.float32).reshape(length, head_count, -1)
    b_heads = jnp.einsum('lgn,hg->lhn', b_full, member, precision=lax.Precision.HIGHEST)
    c_heads = jnp.einsum('lgn,hg->lhn', c_full, member, precision=lax.Precision.HIGHEST)
    step_size = jax.nn.softplus(dt_raw.astype(jnp.float32) + params[0][None, :])
    cumulative = jnp.cumsum(-step_size * jnp.exp(params[1])[None, :], axis=0)
    mixed = state_mixing(x_heads, b_heads, c_heads, step_size, cumulative)
    mixed = mixed + params[2][None, :, None] * x_heads
    gate_act = jax.nn.silu(gate_raw.astype(jnp.float32)).reshape(length, head_count, -1)
    return mixed * gate_act

def reference(hidden, in_weight, out_weight, conv_weight, head_params, packing, head_group):
    inner = HEADS * HEAD_DIM
    width_bc = GROUPS * STATE
    starts = segment_offsets(packing, [inner, inner, width_bc, width_bc, HEADS])
    projected = jnp.dot(hidden, in_weight, preferred_element_type=jnp.float32).astype(jnp.bfloat16)

    def segment(number, extent):
        return lax.dynamic_slice_in_dim(projected, starts[number], extent, 1)
    conv_input = jnp.concatenate([segment(1, inner), segment(2, width_bc), segment(3, width_bc)], axis=1)
    conv_output = causal_conv(conv_input, conv_weight)
    x_values = conv_output[:, :inner]
    b_full = conv_output[:, inner:inner + width_bc].astype(jnp.float32).reshape(SEQ, GROUPS, STATE)
    c_full = conv_output[:, inner + width_bc:].astype(jnp.float32).reshape(SEQ, GROUPS, STATE)
    member = (head_group[:, None] == jnp.arange(GROUPS)[None, :]).astype(jnp.float32)
    gated = gated_heads(segment(0, inner), x_values, b_full, c_full, segment(4, HEADS), head_params, member)
    squares = lax.optimization_barrier(jnp.sum(gated * gated, axis=2))
    group_sq = jnp.dot(squares, member, precision=lax.Precision.HIGHEST)
    group_ms = group_sq / (HEADS // GROUPS * HEAD_DIM)
    per_head = jnp.dot(group_ms, member.T, precision=lax.Precision.HIGHEST)
    normed = (gated * lax.rsqrt(per_head + epsilon)[:, :, None]).reshape(SEQ, inner).astype(jnp.bfloat16)
    return jnp.dot(normed, out_weight, preferred_element_type=jnp.float32).astype(jnp.bfloat16)
```

```python
import functools

import jax
import jax.numpy as jnp
from jax import lax
from jax.experimental import pallas as pl
from jax.experimental.pallas import tpu as pltpu
from jax.sharding import PartitionSpec as P

D = 4096
HEADS = 64
HEAD_DIM = 32
GROUPS = 8
STATE = 128
SEQ = 128
INNER = HEADS * HEAD_DIM
WIDTH_BC = GROUPS * STATE
COLS = 2 * INNER + 2 * WIDTH_BC + HEADS
MEMBERS = 16
CHIPS = MEMBERS // 2
ROWS = D // MEMBERS
HALF = SEQ // 2
PER_GROUP = HEADS // GROUPS
LOCAL = HEADS // MEMBERS
CHANNELS = LOCAL * HEAD_DIM
DT_ROWS = 16
PACKED = 2 * CHANNELS + DT_ROWS

epsilon = 1e-05
F32 = jnp.float32
BF16 = jnp.bfloat16

NT = (((1,), (1,)), ((), ()))


def segment_offsets(packing):
    widths = jnp.where(packing < 2, INNER, jnp.where(packing < 4, WIDTH_BC, HEADS))
    starts = jnp.cumsum(widths) - widths
    numbers = jnp.arange(5)
    return jnp.sum(
        jnp.where(packing[None, :] == numbers[:, None], starts[None, :], 0), axis=1
    ).astype(jnp.int32)


def head_ranks(head_group):
    index = jnp.arange(HEADS)
    before = (head_group[None, :] < head_group[:, None]) | (
        (head_group[None, :] == head_group[:, None]) & (index[None, :] < index[:, None])
    )
    rank = jnp.sum(before.astype(jnp.int32), axis=1)
    order = jnp.sum(
        jnp.where(rank[None, :] == index[:, None], index[None, :], 0), axis=1
    )
    return rank.astype(jnp.int32), order.astype(jnp.int32)


def project_kernel(starts, order, rank, acts, own, peer, out):
    core = lax.axis_index("tensor") % 2
    rows = acts[pl.ds(pl.multiple_of(core * HALF, HALF), HALF), :]
    first, second = rows[:, :ROWS], rows[:, ROWS:]
    is_first = core == 0
    act_own = jnp.where(is_first, first, second)
    act_peer = jnp.where(is_first, second, first)
    act_own = jnp.concatenate([act_own, act_own], axis=0)
    act_peer = jnp.concatenate([act_peer, act_peer], axis=0)

    def multiply(pick):
        return lax.dot_general(
            pick(own), act_own, NT, preferred_element_type=F32
        ) + lax.dot_general(pick(peer), act_peer, NT, preferred_element_type=F32)

    def heads_of(segment, first_head):
        def pick(ref):
            parts = []
            for offset in range(PER_GROUP):
                begin = starts[segment] + order[first_head + offset] * HEAD_DIM
                parts.append(ref[pl.ds(pl.multiple_of(begin, HEAD_DIM), HEAD_DIM), :])
            return jnp.concatenate(parts, axis=0)

        return pick

    def rows_of(segment, begin, extent):
        def pick(ref):
            return ref[pl.ds(pl.multiple_of(starts[segment] + begin, 64), extent), :]

        return pick

    low = lax.broadcasted_iota(jnp.int32, (CHANNELS, SEQ), 1) < HALF

    def chip(index, carry):
        z_part = multiply(heads_of(0, index * PER_GROUP))
        x_part = multiply(heads_of(1, index * PER_GROUP))
        b_part = multiply(rows_of(2, index * STATE, STATE))
        c_part = multiply(rows_of(3, index * STATE, STATE))
        for core_to in range(2):
            picked = slice(core_to * CHANNELS, (core_to + 1) * CHANNELS)
            target = 2 * index + core_to
            out[target, :CHANNELS, :] = jnp.where(low, z_part[picked], b_part).astype(BF16)
            out[target, CHANNELS : 2 * CHANNELS, :] = jnp.where(
                low, x_part[picked], c_part
            ).astype(BF16)
        return carry

    lax.fori_loop(0, CHIPS, chip, 0)

    steps = multiply(rows_of(4, 0, HEADS)).astype(BF16)
    row = lax.broadcasted_iota(jnp.int32, (MEMBERS * DT_ROWS, HEADS), 0)
    inner = row % DT_ROWS
    wanted = jnp.where(inner < LOCAL, (row // DT_ROWS) * LOCAL + inner, -1)
    chosen = (wanted == rank[...]).astype(BF16)
    sorted_steps = jnp.dot(chosen, steps, preferred_element_type=F32).astype(BF16)
    out[:, 2 * CHANNELS :, :] = sorted_steps.reshape(MEMBERS, DT_ROWS, SEQ)


def silu(values):
    return values / (1.0 + jnp.exp(-values))


def mix_kernel(order, params, received, taps_ref, out, taps_scratch):
    member = lax.axis_index("tensor")
    group = member // 2
    heads = [order[member * LOCAL + r] for r in range(LOCAL)]

    halves = []
    for core in range(2):
        total = received[core].astype(F32)
        for chip in range(1, CHIPS):
            total = total + received[2 * chip + core].astype(F32)
        halves.append(total)
    early, late = halves
    lane = lax.broadcasted_iota(jnp.int32, (1, SEQ), 1)
    low = lane < HALF
    main = 2 * CHANNELS
    zx = jnp.where(low, early[:main], pltpu.roll(late[:main], HALF, 1))
    bc = jnp.where(low, pltpu.roll(early[:main], HALF, 1), late[:main])
    steps_raw = jnp.where(low, early[main : main + 8], late[main : main + 8])
    zx = zx.astype(BF16).astype(F32)
    bc = bc.astype(BF16).astype(F32)
    steps_raw = steps_raw.astype(BF16).astype(F32)

    chunks = [
        taps_ref[:, pl.ds(pl.multiple_of((heads[r] // 4) * 128, 128), 128)] for r in range(LOCAL)
    ]
    for base in (INNER, INNER + WIDTH_BC):
        chunks.append(taps_ref[:, pl.ds(pl.multiple_of(base + group * STATE, 128), 128)])
    chunks.append(jnp.zeros((128 - 4 * len(chunks), 128), F32))
    taps_scratch[...] = jnp.concatenate(chunks, axis=0).T

    def conv(values, taps):
        total = taps[:, 3:4] * values
        for tap in range(3):
            shift = 3 - tap
            moved = jnp.where(lane >= shift, pltpu.roll(values, shift, 1), 0.0)
            total = total + taps[:, tap : tap + 1] * moved
        return silu(total).astype(BF16)

    x_taps = jnp.concatenate(
        [
            taps_scratch[pl.ds(pl.multiple_of((heads[r] % 4) * HEAD_DIM, HEAD_DIM), HEAD_DIM), :][
                :, 4 * r : 4 * r + 4
            ]
            for r in range(LOCAL)
        ],
        axis=0,
    )
    x_values = conv(zx[CHANNELS:], x_taps)
    b_values = conv(bc[:CHANNELS], taps_scratch[:, 4 * LOCAL : 4 * LOCAL + 4])
    c_values = conv(bc[CHANNELS:], taps_scratch[:, 4 * LOCAL + 4 : 4 * LOCAL + 8])

    step_rows, rate_rows = [], []
    for r in range(LOCAL):
        raw = steps_raw[r : r + 1] + params[0, heads[r]]
        step = jnp.maximum(raw, 0.0) + jnp.log1p(jnp.exp(-jnp.abs(raw)))
        step_rows.append(step)
        rate_rows.append(-step * jnp.exp(jnp.full((1, SEQ), params[1, heads[r]], F32)))
    running = jnp.concatenate(rate_rows + rate_rows, axis=0)
    for power in range(7):
        shift = 1 << power
        running = running + jnp.where(lane >= shift, pltpu.roll(running, shift, 1), 0.0)
    columns = jnp.concatenate(
        [running[:LOCAL]] + step_rows + [jnp.zeros((128 - 2 * LOCAL, SEQ), F32)], axis=0
    ).T

    scores = lax.dot_general(
        b_values.astype(F32).T.astype(BF16), c_values, (((1,), (0,)), ((), ())),
        preferred_element_type=F32,
    )
    source = lax.broadcasted_iota(jnp.int32, (SEQ, SEQ), 0)
    target = lax.broadcasted_iota(jnp.int32, (SEQ, SEQ), 1)
    causal = source <= target
    gate = silu(zx[:CHANNELS])
    mixed = []
    for r in range(LOCAL):
        spread = running[r : r + 1] - columns[:, r : r + 1]
        decay = jnp.where(causal, jnp.exp(jnp.where(causal, spread, 0.0)), 0.0)
        weights = (decay * scores * columns[:, LOCAL + r : LOCAL + r + 1]).astype(BF16)
        x_head = x_values[r * HEAD_DIM : (r + 1) * HEAD_DIM]
        y_head = jnp.dot(x_head, weights, preferred_element_type=F32)
        mixed.append(y_head + params[2, heads[r]] * x_head.astype(F32))
    gated = jnp.concatenate(mixed, axis=0) * gate
    result = gated.T.astype(BF16)
    for index in range(MEMBERS):
        out[index] = result


def finish_kernel(order, gathered, weight, out):
    total = jnp.zeros((SEQ, ROWS), F32)
    for group in range(GROUPS):
        values = jnp.concatenate([gathered[2 * group], gathered[2 * group + 1]], axis=1)
        wide = values.astype(F32)
        mean_square = jnp.sum(wide * wide, axis=1, keepdims=True) / (PER_GROUP * HEAD_DIM)
        parts = []
        for offset in range(PER_GROUP):
            begin = order[group * PER_GROUP + offset] * HEAD_DIM
            parts.append(weight[pl.ds(pl.multiple_of(begin, HEAD_DIM), HEAD_DIM), :])
        product = jnp.dot(values, jnp.concatenate(parts, axis=0), preferred_element_type=F32)
        total = total + product * lax.rsqrt(mean_square + epsilon)
    out[...] = total.astype(BF16)


SMEM = pl.BlockSpec(memory_space=pltpu.SMEM)
VMEM = pl.BlockSpec(memory_space=pltpu.VMEM)


def shards(hidden, in_weight, out_weight, conv_weight, head_params, packing, head_group):
    starts = segment_offsets(packing)
    rank, order = head_ranks(head_group)

    own = in_weight.T
    peer = lax.ppermute(own, "tensor", [(i, i ^ 1) for i in range(MEMBERS)])
    per_chip = hidden.reshape(8, CHIPS, 2 * ROWS).transpose(1, 0, 2)
    outgoing = jnp.broadcast_to(per_chip[:, None], (CHIPS, 2, 8, 2 * ROWS))
    acts = lax.all_to_all(
        outgoing.reshape(MEMBERS, 8, 2 * ROWS), "tensor", split_axis=0, concat_axis=0, tiled=True
    ).reshape(SEQ, 2 * ROWS)

    partial = pl.pallas_call(
        project_kernel,
        out_shape=jax.ShapeDtypeStruct((MEMBERS, PACKED, SEQ), BF16),
        in_specs=[SMEM, SMEM, VMEM, VMEM, VMEM, VMEM],
        out_specs=VMEM,
        compiler_params=pltpu.CompilerParams(vmem_limit_bytes=20 * 1024 * 1024),
        name="project",
    )(starts, order, rank.reshape(1, HEADS), acts, own, peer)
    received = lax.all_to_all(partial, "tensor", split_axis=0, concat_axis=0, tiled=True)

    gated = pl.pallas_call(
        mix_kernel,
        out_shape=jax.ShapeDtypeStruct((MEMBERS, SEQ, CHANNELS), BF16),
        in_specs=[SMEM, SMEM, VMEM, VMEM],
        out_specs=VMEM,
        scratch_shapes=[pltpu.VMEM((128, 128), F32)],
        compiler_params=pltpu.CompilerParams(vmem_limit_bytes=16 * 1024 * 1024),
        name="mix",
    )(order, head_params, received, conv_weight)
    gathered = lax.all_to_all(gated, "tensor", split_axis=0, concat_axis=0, tiled=True)

    share = pl.pallas_call(
        finish_kernel,
        out_shape=jax.ShapeDtypeStruct((SEQ, ROWS), BF16),
        in_specs=[SMEM, VMEM, VMEM],
        out_specs=VMEM,
        compiler_params=pltpu.CompilerParams(vmem_limit_bytes=16 * 1024 * 1024),
        name="finish",
    )(order, gathered, out_weight)
    pieces = lax.all_to_all(
        share.reshape(MEMBERS, SEQ // MEMBERS, ROWS), "tensor", split_axis=0, concat_axis=0, tiled=True
    )
    return pieces.transpose(1, 0, 2).reshape(SEQ // MEMBERS, D)


def solution(mesh):
    in_specs = (P(("dp", "tensor"), None), P("tensor", None), P(None, "tensor"), P(), P(), P(), P())
    out_specs = P(("dp", "tensor"), None)
    return jax.shard_map(shards, mesh=mesh, in_specs=in_specs, out_specs=out_specs, check_vma=False)
```

```python
import functools

import jax
import jax.numpy as jnp
from jax import lax
from jax.experimental import pallas as pl
from jax.experimental.pallas import tpu as pltpu
from jax.sharding import PartitionSpec as P

D = 4096
HEADS = 64
HEAD_DIM = 32
GROUPS = 8
STATE = 128
SEQ = 128
INNER = HEADS * HEAD_DIM
WIDTH_BC = GROUPS * STATE
COLS = 2 * INNER + 2 * WIDTH_BC + HEADS
MEMBERS = 16
CHIPS = MEMBERS // 2
ROWS = D // MEMBERS
HALF = SEQ // 2
PER_GROUP = HEADS // GROUPS
LOCAL = HEADS // MEMBERS
CHANNELS = LOCAL * HEAD_DIM
DT_ROWS = 16
PACKED = 2 * CHANNELS + DT_ROWS

epsilon = 1e-05
F32 = jnp.float32
BF16 = jnp.bfloat16

NT = (((1,), (1,)), ((), ()))


CHIP_GROUPS = [[2 * chip + core for chip in range(CHIPS)] for core in range(2)]
ORDER, STARTS = 0, HEADS


def stage_kernel(packing, head_group, plan, arrange, filled):
    begin = jnp.int32(0)
    for place in range(5):
        number = packing[place]
        plan[STARTS + number] = begin
        begin = begin + jnp.where(number < 2, INNER, jnp.where(number < 4, WIDTH_BC, HEADS))
    for spare in range(STARTS + 5, 80):
        plan[spare] = 0
    for group in range(GROUPS):
        filled[group] = 0

    def place_head(head, carry):
        group = head_group[head]
        position = filled[group]
        plan[ORDER + group * PER_GROUP + position] = head
        filled[group] = position + 1
        return carry

    lax.fori_loop(0, HEADS, place_head, 0, unroll=8)

    source = lax.broadcasted_iota(jnp.int32, (2 * SEQ, 2 * SEQ), 0)
    target = lax.broadcasted_iota(jnp.int32, (2 * SEQ, 2 * SEQ), 1)
    column = source % HALF
    token = 16 * (column // 8) + 8 * (source // SEQ) + column % 8
    wanted = token + SEQ * ((source // HALF) % 2)
    arrange[...] = jnp.where(wanted == target, 1.0, 0.0).astype(BF16)


def project_kernel(plan, acts, own, peer, out, steps_ref, sorted_ref):
    core = lax.axis_index("tensor") % 2
    rows = acts[...]
    first, second = rows[:, :ROWS], rows[:, ROWS:]
    is_first = core == 0
    both = jnp.concatenate(
        [jnp.where(is_first, first, second), jnp.where(is_first, second, first)], axis=1
    )
    both = jnp.concatenate([both, both], axis=0)

    def multiply(begins, extent):
        picked = []
        for begin in begins:
            where = pl.ds(pl.multiple_of(begin, HEAD_DIM), extent)
            picked.append(jnp.concatenate([own[where, :], peer[where, :]], axis=1))
        return lax.dot_general(
            jnp.concatenate(picked, axis=0), both, NT, preferred_element_type=F32
        )

    steps_ref[...] = multiply([plan[STARTS + 4]], HEADS)
    sorted_ref[...] = jnp.zeros_like(sorted_ref)
    for member in range(MEMBERS):
        for r in range(LOCAL):
            sorted_ref[pl.ds(member * DT_ROWS + r, 1), :] = steps_ref[
                pl.ds(plan[ORDER + member * LOCAL + r], 1), :
            ]
    out[:, 2 * CHANNELS :, :] = sorted_ref[...].astype(BF16).reshape(MEMBERS, DT_ROWS, SEQ)

    low = lax.broadcasted_iota(jnp.int32, (CHANNELS, SEQ), 1) < HALF

    def chip(index, carry):
        heads = [plan[ORDER + index * PER_GROUP + offset] for offset in range(PER_GROUP)]
        z_part = multiply([plan[STARTS] + head * HEAD_DIM for head in heads], HEAD_DIM)
        x_part = multiply([plan[STARTS + 1] + head * HEAD_DIM for head in heads], HEAD_DIM)
        bc_part = multiply([plan[STARTS + 2] + index * STATE, plan[STARTS + 3] + index * STATE], STATE)
        for core_to in range(2):
            picked = slice(core_to * CHANNELS, (core_to + 1) * CHANNELS)
            target = 2 * index + core_to
            out[target, :CHANNELS, :] = jnp.where(
                low, z_part[picked], bc_part[:STATE]
            ).astype(BF16)
            out[target, CHANNELS : 2 * CHANNELS, :] = jnp.where(
                low, x_part[picked], bc_part[STATE:]
            ).astype(BF16)
        return carry

    lax.fori_loop(0, CHIPS, chip, 0, unroll=2)


def silu(values):
    return values / (1.0 + jnp.exp(-values))


def mix_kernel(plan, params, received, taps_ref, arrange, out, taps_scratch):
    member = lax.axis_index("tensor")
    group = member // 2
    heads = [plan[ORDER + member * LOCAL + r] for r in range(LOCAL)]

    halves = []
    for core in range(2):
        total = received[core].astype(F32)
        for chip in range(1, CHIPS):
            total = total + received[2 * chip + core].astype(F32)
        halves.append(total)
    lane = lax.broadcasted_iota(jnp.int32, (1, SEQ), 1)
    summed = jnp.concatenate([half.astype(BF16) for half in halves], axis=1)
    ordered = jnp.dot(summed, arrange[...], preferred_element_type=F32)
    zx = ordered[: 2 * CHANNELS, :SEQ]
    bc = ordered[: 2 * CHANNELS, SEQ:]
    steps_raw = ordered[2 * CHANNELS :, :SEQ]

    chunks = [
        taps_ref[:, pl.ds(pl.multiple_of((heads[r] // 4) * 128, 128), 128)] for r in range(LOCAL)
    ]
    for base in (INNER, INNER + WIDTH_BC):
        chunks.append(taps_ref[:, pl.ds(pl.multiple_of(base + group * STATE, 128), 128)])
    chunks.append(jnp.zeros((128 - 4 * len(chunks), 128), F32))
    taps_scratch[...] = jnp.concatenate(chunks, axis=0).T

    def conv(values, taps):
        total = taps[:, 3:4] * values
        for tap in range(3):
            shift = 3 - tap
            moved = jnp.where(lane >= shift, pltpu.roll(values, shift, 1), 0.0)
            total = total + taps[:, tap : tap + 1] * moved
        return silu(total).astype(BF16)

    x_taps = jnp.concatenate(
        [
            taps_scratch[pl.ds(pl.multiple_of((heads[r] % 4) * HEAD_DIM, HEAD_DIM), HEAD_DIM), :][
                :, 4 * r : 4 * r + 4
            ]
            for r in range(LOCAL)
        ],
        axis=0,
    )
    x_values = conv(zx[CHANNELS:], x_taps)
    b_values = conv(bc[:CHANNELS], taps_scratch[:, 4 * LOCAL : 4 * LOCAL + 4])
    c_values = conv(bc[CHANNELS:], taps_scratch[:, 4 * LOCAL + 4 : 4 * LOCAL + 8])

    step_rows, rate_rows = [], []
    for r in range(LOCAL):
        raw = steps_raw[r : r + 1] + params[0, heads[r]]
        step = jnp.maximum(raw, 0.0) + jnp.log1p(jnp.exp(-jnp.abs(raw)))
        step_rows.append(step)
        rate_rows.append(-step * jnp.exp(jnp.full((1, SEQ), params[1, heads[r]], F32)))
    running = jnp.concatenate(rate_rows + rate_rows, axis=0)
    for power in range(7):
        shift = 1 << power
        running = running + jnp.where(lane >= shift, pltpu.roll(running, shift, 1), 0.0)
    columns = jnp.concatenate(
        [running[:LOCAL]] + step_rows + [jnp.zeros((128 - 2 * LOCAL, SEQ), F32)], axis=0
    ).T

    scores = lax.dot_general(
        b_values.astype(F32).T.astype(BF16), c_values, (((1,), (0,)), ((), ())),
        preferred_element_type=F32,
    )
    source = lax.broadcasted_iota(jnp.int32, (SEQ, SEQ), 0)
    target = lax.broadcasted_iota(jnp.int32, (SEQ, SEQ), 1)
    causal = source <= target
    gate = silu(zx[:CHANNELS])
    mixed = []
    for r in range(LOCAL):
        spread = running[r : r + 1] - columns[:, r : r + 1]
        decay = jnp.where(causal, jnp.exp(jnp.where(causal, spread, 0.0)), 0.0)
        weights = (decay * scores * columns[:, LOCAL + r : LOCAL + r + 1]).astype(BF16)
        x_head = x_values[r * HEAD_DIM : (r + 1) * HEAD_DIM]
        y_head = jnp.dot(x_head, weights, preferred_element_type=F32)
        mixed.append(y_head + params[2, heads[r]] * x_head.astype(F32))
    gated = jnp.concatenate(mixed, axis=0) * gate
    result = gated.T.astype(BF16)
    for index in range(MEMBERS):
        out[index] = result


def finish_kernel(plan, gathered, weight, out):
    total = jnp.zeros((SEQ, ROWS), F32)
    for group in range(GROUPS):
        values = jnp.concatenate([gathered[2 * group], gathered[2 * group + 1]], axis=1)
        wide = values.astype(F32)
        mean_square = jnp.sum(wide * wide, axis=1, keepdims=True) / (PER_GROUP * HEAD_DIM)
        parts = []
        for offset in range(PER_GROUP):
            begin = plan[ORDER + group * PER_GROUP + offset] * HEAD_DIM
            parts.append(weight[pl.ds(pl.multiple_of(begin, HEAD_DIM), HEAD_DIM), :])
        product = jnp.dot(values, jnp.concatenate(parts, axis=0), preferred_element_type=F32)
        total = total + product * lax.rsqrt(mean_square + epsilon)
    out[...] = total.astype(BF16)


SMEM = pl.BlockSpec(memory_space=pltpu.SMEM)
VMEM = pl.BlockSpec(memory_space=pltpu.VMEM)


def shards(hidden, in_weight, out_weight, conv_weight, head_params, packing, head_group):
    own = in_weight.T
    peer = lax.ppermute(own, "tensor", [(i, i ^ 1) for i in range(MEMBERS)])
    per_chip = hidden.reshape(SEQ // MEMBERS, CHIPS, 2 * ROWS).transpose(1, 0, 2)
    acts = lax.all_to_all(
        per_chip, "tensor", split_axis=0, concat_axis=0, tiled=True, axis_index_groups=CHIP_GROUPS
    ).reshape(HALF, 2 * ROWS)

    plan, arrange = pl.pallas_call(
        stage_kernel,
        out_shape=(
            jax.ShapeDtypeStruct((80,), jnp.int32),
            jax.ShapeDtypeStruct((2 * SEQ, 2 * SEQ), BF16),
        ),
        in_specs=[SMEM, SMEM],
        out_specs=(SMEM, VMEM),
        scratch_shapes=[pltpu.SMEM((GROUPS,), jnp.int32)],
        compiler_params=pltpu.CompilerParams(vmem_limit_bytes=2 * 1024 * 1024),
        cost_estimate=pl.CostEstimate(flops=4 * 10**9, bytes_accessed=4 * 10**6, transcendentals=0),
        name="stage",
    )(packing, head_group)

    partial = pl.pallas_call(
        project_kernel,
        out_shape=jax.ShapeDtypeStruct((MEMBERS, PACKED, SEQ), BF16),
        in_specs=[SMEM, VMEM, VMEM, VMEM],
        out_specs=VMEM,
        scratch_shapes=[pltpu.VMEM((HEADS, SEQ), F32), pltpu.VMEM((MEMBERS * DT_ROWS, SEQ), F32)],
        compiler_params=pltpu.CompilerParams(vmem_limit_bytes=16 * 1024 * 1024),
        name="project",
    )(plan, acts, own, peer)
    received = lax.all_to_all(partial, "tensor", split_axis=0, concat_axis=0, tiled=True)

    gated = pl.pallas_call(
        mix_kernel,
        out_shape=jax.ShapeDtypeStruct((MEMBERS, SEQ, CHANNELS), BF16),
        in_specs=[SMEM, SMEM, VMEM, VMEM, VMEM],
        out_specs=VMEM,
        scratch_shapes=[pltpu.VMEM((128, 128), F32)],
        compiler_params=pltpu.CompilerParams(vmem_limit_bytes=8 * 1024 * 1024),
        name="mix",
    )(plan, head_params, received, conv_weight, arrange)
    gathered = lax.all_to_all(gated, "tensor", split_axis=0, concat_axis=0, tiled=True)

    share = pl.pallas_call(
        finish_kernel,
        out_shape=jax.ShapeDtypeStruct((SEQ, ROWS), BF16),
        in_specs=[SMEM, VMEM, VMEM],
        out_specs=VMEM,
        compiler_params=pltpu.CompilerParams(vmem_limit_bytes=8 * 1024 * 1024),
        name="finish",
    )(plan, gathered, out_weight)
    pieces = lax.all_to_all(
        share.reshape(MEMBERS, SEQ // MEMBERS, ROWS), "tensor", split_axis=0, concat_axis=0, tiled=True
    )
    return pieces.transpose(1, 0, 2).reshape(SEQ // MEMBERS, D)


def solution(mesh):
    in_specs = (P(("dp", "tensor"), None), P("tensor", None), P(None, "tensor"), P(), P(), P(), P())
    out_specs = P(("dp", "tensor"), None)
    return jax.shard_map(shards, mesh=mesh, in_specs=in_specs, out_specs=out_specs, check_vma=False)
```

```python
import functools

import jax
import jax.numpy as jnp
from jax import lax
from jax.experimental import pallas as pl
from jax.experimental.pallas import tpu as pltpu
from jax.sharding import PartitionSpec as P

D = 4096
HEADS = 64
HEAD_DIM = 32
GROUPS = 8
STATE = 128
SEQ = 128
INNER = HEADS * HEAD_DIM
WIDTH_BC = GROUPS * STATE
COLS = 2 * INNER + 2 * WIDTH_BC + HEADS
MEMBERS = 16
CHIPS = MEMBERS // 2
ROWS = D // MEMBERS
HALF = SEQ // 2
PER_GROUP = HEADS // GROUPS
LOCAL = HEADS // MEMBERS
CHANNELS = LOCAL * HEAD_DIM
DT_ROWS = 16
PACKED = 2 * CHANNELS + DT_ROWS

epsilon = 1e-05
F32 = jnp.float32
BF16 = jnp.bfloat16

NT = (((1,), (1,)), ((), ()))


CORE_SWAP = [(member, member ^ 1) for member in range(MEMBERS)]
CHIP_GROUPS = [[2 * chip + core for chip in range(CHIPS)] for core in range(2)]
ORDER, STARTS = 0, HEADS


def arrange_kernel(arrange):
    source = lax.broadcasted_iota(jnp.int32, (2 * SEQ, 2 * SEQ), 0)
    target = lax.broadcasted_iota(jnp.int32, (2 * SEQ, 2 * SEQ), 1)
    column = source % HALF
    token = 16 * (column // 8) + 8 * (source // SEQ) + column % 8
    wanted = token + SEQ * ((source // HALF) % 2)
    arrange[...] = jnp.where(wanted == target, 1.0, 0.0).astype(BF16)


def slot_of(member):
    return (2 * (member // 4) + member % 2) * 2 + (member // 2) % 2


def project_kernel(packing, head_group, acts, own, peer, _, out, plan, steps_ref, sorted_ref):
    begin = jnp.int32(0)
    for place in range(5):
        number = packing[place]
        plan[STARTS + number] = begin
        begin = begin + jnp.where(number < 2, INNER, jnp.where(number < 4, WIDTH_BC, HEADS))
    for spare in range(STARTS + 5, 80):
        plan[spare] = 0
    filled = jnp.int32(0)
    for head in range(HEADS):
        group = head_group[head]
        position = lax.shift_right_logical(filled, 4 * group) & 15
        plan[ORDER + group * PER_GROUP + position] = head
        filled = filled + lax.shift_left(jnp.int32(1), 4 * group)

    rows = acts[...]
    is_first = lax.axis_index("tensor") % 2 == 0
    first, second = rows[:, :ROWS], rows[:, ROWS:]
    both = jnp.concatenate(
        [jnp.where(is_first, first, second), jnp.where(is_first, second, first)], axis=1
    )
    both = jnp.concatenate([both, both], axis=0).astype(F32).T.astype(BF16)
    low = lax.broadcasted_iota(jnp.int32, (CHANNELS, SEQ), 1) < HALF

    def taken(number, begin, extent):
        where = pl.ds(pl.multiple_of(plan[STARTS + number] + begin, HEAD_DIM), extent)
        return jnp.concatenate([own[where, :], peer[where, :]], axis=1)

    for group in range(GROUPS):
        heads = [plan[ORDER + group * PER_GROUP + offset] for offset in range(PER_GROUP)]
        weights = jnp.concatenate(
            [taken(number, head * HEAD_DIM, HEAD_DIM) for number in range(2) for head in heads]
            + [taken(number, group * STATE, STATE) for number in range(2, 4)],
            axis=0,
        )
        parts = jnp.dot(weights, both, preferred_element_type=F32)
        for side in range(2):
            target = 4 * (group // 2) + 2 * side + group % 2
            for number in range(2):
                begin = (2 * number + side) * CHANNELS
                other = (4 + number) * CHANNELS
                out[target, number * CHANNELS : (number + 1) * CHANNELS, :] = jnp.where(
                    low, parts[begin : begin + CHANNELS], parts[other : other + CHANNELS]
                ).astype(BF16)

    steps_ref[...] = jnp.dot(taken(4, 0, HEADS), both, preferred_element_type=F32)
    sorted_ref[...] = jnp.zeros_like(sorted_ref)
    for member in range(MEMBERS):
        for r in range(LOCAL):
            sorted_ref[pl.ds(member * DT_ROWS + r, 1), :] = steps_ref[
                pl.ds(plan[ORDER + slot_of(member) * LOCAL + r], 1), :
            ]
    out[:, 2 * CHANNELS :, :] = sorted_ref[...].astype(BF16).reshape(MEMBERS, DT_ROWS, SEQ)


def silu(values):
    return values / (1.0 + jnp.exp(-values))


def mix_kernel(plan, params, received, taps_ref, arrange, swapped, out, held, taps_scratch, arrived):
    fetch = pltpu.make_async_copy(swapped, held, arrived)
    fetch.start()
    member = lax.axis_index("tensor")
    slot = slot_of(member)
    group = slot // 2
    heads = [plan[ORDER + slot * LOCAL + r] for r in range(LOCAL)]

    halves = []
    for core in range(2):
        total = received[core].astype(F32)
        for chip in range(1, CHIPS):
            total = total + received[2 * chip + core].astype(F32)
        halves.append(total)
    lane = lax.broadcasted_iota(jnp.int32, (1, SEQ), 1)
    summed = jnp.concatenate([half.astype(BF16) for half in halves], axis=1)
    ordered = jnp.dot(summed, arrange[...], preferred_element_type=F32)
    zx = ordered[: 2 * CHANNELS, :SEQ]
    bc = ordered[: 2 * CHANNELS, SEQ:]
    steps_raw = ordered[2 * CHANNELS :, :SEQ]

    chunks = [
        taps_ref[:, pl.ds(pl.multiple_of((heads[r] // 4) * 128, 128), 128)] for r in range(LOCAL)
    ]
    for base in (INNER, INNER + WIDTH_BC):
        chunks.append(taps_ref[:, pl.ds(pl.multiple_of(base + group * STATE, 128), 128)])
    chunks.append(jnp.zeros((128 - 4 * len(chunks), 128), F32))
    taps_scratch[...] = jnp.concatenate(chunks, axis=0).T

    def conv(values, taps):
        total = taps[:, 3:4] * values
        for tap in range(3):
            shift = 3 - tap
            moved = jnp.where(lane >= shift, pltpu.roll(values, shift, 1), 0.0)
            total = total + taps[:, tap : tap + 1] * moved
        return silu(total).astype(BF16)

    x_taps = jnp.concatenate(
        [
            taps_scratch[pl.ds(pl.multiple_of((heads[r] % 4) * HEAD_DIM, HEAD_DIM), HEAD_DIM), :][
                :, 4 * r : 4 * r + 4
            ]
            for r in range(LOCAL)
        ],
        axis=0,
    )
    x_values = conv(zx[CHANNELS:], x_taps)
    b_values = conv(bc[:CHANNELS], taps_scratch[:, 4 * LOCAL : 4 * LOCAL + 4])
    c_values = conv(bc[CHANNELS:], taps_scratch[:, 4 * LOCAL + 4 : 4 * LOCAL + 8])

    row = lax.broadcasted_iota(jnp.int32, (2 * LOCAL, SEQ), 0)

    def per_head(number):
        values = jnp.zeros((2 * LOCAL, SEQ), F32)
        for r in range(LOCAL):
            values = jnp.where(row == r, params[number, heads[r]], values)
        return values

    raw = steps_raw[: 2 * LOCAL] + per_head(0)
    steps = jnp.maximum(raw, 0.0) + jnp.log1p(jnp.exp(-jnp.abs(raw)))
    rates = -steps * jnp.exp(per_head(1))
    high = rates.astype(BF16)
    rest = rates - high.astype(F32)
    middle = rest.astype(BF16)
    low = (rest - middle.astype(F32)).astype(BF16)
    source = lax.broadcasted_iota(jnp.int32, (SEQ, SEQ), 0)
    target = lax.broadcasted_iota(jnp.int32, (SEQ, SEQ), 1)
    causal = source <= target
    until = jnp.where(causal, 1.0, 0.0).astype(BF16)
    parts = jnp.dot(jnp.concatenate([high, middle, low, low], axis=0), until, preferred_element_type=F32)
    running = parts[:8] + parts[8:16] + parts[16:24]
    columns = jnp.concatenate(
        [running[:LOCAL], steps[:LOCAL], jnp.zeros((128 - 2 * LOCAL, SEQ), F32)], axis=0
    ).T

    scores = lax.dot_general(
        b_values.astype(F32).T.astype(BF16), c_values, (((1,), (0,)), ((), ())),
        preferred_element_type=F32,
    )
    gate = silu(zx[:CHANNELS])
    mixed = []
    for r in range(LOCAL):
        spread = running[r : r + 1] - columns[:, r : r + 1]
        decay = jnp.exp(jnp.where(causal, spread, -1e30))
        weights = (decay * scores * columns[:, LOCAL + r : LOCAL + r + 1]).astype(BF16)
        x_head = x_values[r * HEAD_DIM : (r + 1) * HEAD_DIM]
        y_head = jnp.dot(x_head, weights, preferred_element_type=F32)
        mixed.append(y_head + params[2, heads[r]] * x_head.astype(F32))
    gated = jnp.concatenate(mixed, axis=0) * gate
    result = gated.T.astype(BF16)
    for index in range(CHIPS):
        out[index] = result
    fetch.wait()


def finish_kernel(plan, gathered, own, peer, out):
    core = lax.axis_index("tensor") % 2
    normed, begins = [], []
    for row in range(4):
        values = jnp.concatenate([gathered[2 * row], gathered[2 * row + 1]], axis=1).astype(F32)
        mean_square = jnp.sum(values * values, axis=1, keepdims=True) / (PER_GROUP * HEAD_DIM)
        normed.append((values * lax.rsqrt(mean_square + epsilon)).astype(BF16))
        for offset in range(PER_GROUP):
            begins.append(plan[ORDER + (2 * row + core) * PER_GROUP + offset] * HEAD_DIM)
    normed = jnp.concatenate(normed, axis=1)

    def columns(ref, place):
        rows = [ref[pl.ds(pl.multiple_of(begin, HEAD_DIM), HEAD_DIM), :] for begin in begins]
        product = jnp.dot(normed, jnp.concatenate(rows, axis=0), preferred_element_type=F32)
        out[:, :, pl.ds(pl.multiple_of(place * ROWS, ROWS), ROWS)] = product.astype(BF16).reshape(
            MEMBERS, SEQ // MEMBERS, ROWS
        )

    columns(own, core)
    columns(peer, 1 - core)


def combine_kernel(received, out):
    for chip in range(CHIPS):
        total = received[2 * chip].astype(F32) + received[2 * chip + 1].astype(F32)
        out[:, 2 * chip * ROWS : (2 * chip + 2) * ROWS] = total.astype(BF16)


SMEM = pl.BlockSpec(memory_space=pltpu.SMEM)
VMEM = pl.BlockSpec(memory_space=pltpu.VMEM)


def shards(hidden, in_weight, out_weight, conv_weight, head_params, packing, head_group):
    own = in_weight.T
    peer = lax.ppermute(own, "tensor", CORE_SWAP)
    per_chip = hidden.reshape(SEQ // MEMBERS, CHIPS, 2 * ROWS).transpose(1, 0, 2)
    acts = lax.all_to_all(
        per_chip, "tensor", split_axis=0, concat_axis=0, tiled=True, axis_index_groups=CHIP_GROUPS
    ).reshape(HALF, 2 * ROWS)

    arrange = pl.pallas_call(
        arrange_kernel,
        out_shape=jax.ShapeDtypeStruct((2 * SEQ, 2 * SEQ), BF16),
        out_specs=VMEM,
        compiler_params=pltpu.CompilerParams(vmem_limit_bytes=2 * 1024 * 1024),
        cost_estimate=pl.CostEstimate(flops=12 * 10**9, bytes_accessed=4 * 10**6, transcendentals=0),
        name="arrange",
    )()
    swapped = lax.ppermute(out_weight, "tensor", CORE_SWAP)

    partial, plan = pl.pallas_call(
        project_kernel,
        out_shape=(
            jax.ShapeDtypeStruct((MEMBERS, PACKED, SEQ), BF16),
            jax.ShapeDtypeStruct((80,), jnp.int32),
        ),
        in_specs=[SMEM, SMEM, VMEM, VMEM, VMEM, pl.BlockSpec(memory_space=pl.ANY)],
        out_specs=(VMEM, SMEM),
        scratch_shapes=[pltpu.VMEM((HEADS, SEQ), F32), pltpu.VMEM((MEMBERS * DT_ROWS, SEQ), F32)],
        compiler_params=pltpu.CompilerParams(vmem_limit_bytes=16 * 1024 * 1024),
        name="project",
    )(packing, head_group, acts, own, peer, arrange)
    partial, swapped = lax.optimization_barrier((partial, swapped))
    received = lax.all_to_all(partial, "tensor", split_axis=0, concat_axis=0, tiled=True)

    gated, held = pl.pallas_call(
        mix_kernel,
        out_shape=(
            jax.ShapeDtypeStruct((CHIPS, SEQ, CHANNELS), BF16),
            jax.ShapeDtypeStruct((INNER, ROWS), BF16),
        ),
        in_specs=[SMEM, SMEM, VMEM, VMEM, VMEM, pl.BlockSpec(memory_space=pl.ANY)],
        out_specs=(VMEM, VMEM),
        scratch_shapes=[pltpu.VMEM((128, 128), F32), pltpu.SemaphoreType.DMA(())],
        compiler_params=pltpu.CompilerParams(vmem_limit_bytes=8 * 1024 * 1024),
        name="mix",
    )(plan, head_params, received, conv_weight, arrange, swapped)
    gathered = lax.all_to_all(
        gated, "tensor", split_axis=0, concat_axis=0, tiled=True, axis_index_groups=CHIP_GROUPS
    )

    share = pl.pallas_call(
        finish_kernel,
        out_shape=jax.ShapeDtypeStruct((MEMBERS, SEQ // MEMBERS, 2 * ROWS), BF16),
        in_specs=[SMEM, VMEM, VMEM, VMEM],
        out_specs=VMEM,
        compiler_params=pltpu.CompilerParams(vmem_limit_bytes=8 * 1024 * 1024),
        name="finish",
    )(plan, gathered, out_weight, held)
    pieces = lax.all_to_all(share, "tensor", split_axis=0, concat_axis=0, tiled=True)
    return pl.pallas_call(
        combine_kernel,
        out_shape=jax.ShapeDtypeStruct((SEQ // MEMBERS, D), BF16),
        in_specs=[VMEM],
        out_specs=VMEM,
        compiler_params=pltpu.CompilerParams(vmem_limit_bytes=4 * 1024 * 1024),
        name="combine",
    )(pieces)


def solution(mesh):
    in_specs = (P(("dp", "tensor"), None), P("tensor", None), P(None, "tensor"), P(), P(), P(), P())
    out_specs = P(("dp", "tensor"), None)
    return jax.shard_map(shards, mesh=mesh, in_specs=in_specs, out_specs=out_specs, check_vma=False)
```

```python
import functools

import jax
import jax.numpy as jnp
from jax import lax
from jax.experimental import pallas as pl
from jax.experimental.pallas import tpu as pltpu
from jax.sharding import PartitionSpec as P

D = 4096
HEADS = 64
HEAD_DIM = 32
GROUPS = 8
STATE = 128
SEQ = 128
INNER = HEADS * HEAD_DIM
WIDTH_BC = GROUPS * STATE
COLS = 2 * INNER + 2 * WIDTH_BC + HEADS
MEMBERS = 16
CHIPS = MEMBERS // 2
ROWS = D // MEMBERS
HALF = SEQ // 2
PER_GROUP = HEADS // GROUPS
LOCAL = HEADS // MEMBERS
CHANNELS = LOCAL * HEAD_DIM
DT_ROWS = 16
PACKED = 2 * CHANNELS + DT_ROWS

epsilon = 1e-05
F32 = jnp.float32
BF16 = jnp.bfloat16

NT = (((1,), (1,)), ((), ()))


CORE_SWAP = [(member, member ^ 1) for member in range(MEMBERS)]
CHIP_GROUPS = [[2 * chip + core for chip in range(CHIPS)] for core in range(2)]
ORDER, STARTS = 0, HEADS


def arrange_kernel(arrange):
    source = lax.broadcasted_iota(jnp.int32, (2 * SEQ, 2 * SEQ), 0)
    target = lax.broadcasted_iota(jnp.int32, (2 * SEQ, 2 * SEQ), 1)
    column = source % HALF
    token = 16 * (column // 8) + 8 * (source // SEQ) + column % 8
    wanted = token + SEQ * ((source // HALF) % 2)
    arrange[...] = jnp.where(wanted == target, 1.0, 0.0).astype(BF16)


def slot_of(member):
    return (2 * (member // 4) + member % 2) * 2 + (member // 2) % 2


def project_kernel(packing, head_group, acts, own, peer, _, out, plan, steps_ref, sorted_ref):
    begin = jnp.int32(0)
    for place in range(5):
        number = packing[place]
        plan[STARTS + number] = begin
        begin = begin + jnp.where(number < 2, INNER, jnp.where(number < 4, WIDTH_BC, HEADS))
    for spare in range(STARTS + 5, 80):
        plan[spare] = 0
    filled = jnp.int32(0)
    for head in range(HEADS):
        group = head_group[head]
        position = lax.shift_right_logical(filled, 4 * group) & 15
        plan[ORDER + group * PER_GROUP + position] = head
        filled = filled + lax.shift_left(jnp.int32(1), 4 * group)

    rows = acts[...]
    is_first = lax.axis_index("tensor") % 2 == 0
    first, second = rows[:, :ROWS], rows[:, ROWS:]
    both = jnp.concatenate(
        [jnp.where(is_first, first, second), jnp.where(is_first, second, first)], axis=1
    )
    both = jnp.concatenate([both, both], axis=0).astype(F32).T.astype(BF16)
    low = lax.broadcasted_iota(jnp.int32, (CHANNELS, SEQ), 1) < HALF

    def taken(number, begin, extent):
        where = pl.ds(pl.multiple_of(plan[STARTS + number] + begin, HEAD_DIM), extent)
        return jnp.concatenate([own[where, :], peer[where, :]], axis=1)

    for group in range(GROUPS):
        heads = [plan[ORDER + group * PER_GROUP + offset] for offset in range(PER_GROUP)]
        weights = jnp.concatenate(
            [taken(number, head * HEAD_DIM, HEAD_DIM) for number in range(2) for head in heads]
            + [taken(number, group * STATE, STATE) for number in range(2, 4)],
            axis=0,
        )
        parts = jnp.dot(weights, both, preferred_element_type=F32)
        for side in range(2):
            target = 4 * (group // 2) + 2 * side + group % 2
            for number in range(2):
                begin = (2 * number + side) * CHANNELS
                other = (4 + number) * CHANNELS
                out[target, number * CHANNELS : (number + 1) * CHANNELS, :] = jnp.where(
                    low, parts[begin : begin + CHANNELS], parts[other : other + CHANNELS]
                ).astype(BF16)

    steps_ref[...] = jnp.dot(taken(4, 0, HEADS), both, preferred_element_type=F32)
    sorted_ref[...] = jnp.zeros_like(sorted_ref)
    for member in range(MEMBERS):
        for r in range(LOCAL):
            sorted_ref[pl.ds(member * DT_ROWS + r, 1), :] = steps_ref[
                pl.ds(plan[ORDER + slot_of(member) * LOCAL + r], 1), :
            ]
    out[:, 2 * CHANNELS :, :] = sorted_ref[...].astype(BF16).reshape(MEMBERS, DT_ROWS, SEQ)


def silu(values):
    return values / (1.0 + jnp.exp(-values))


def mix_kernel(
    plan_ref, params_ref, received, taps_ref, arrange, swapped, out, held, taps_scratch, plan, params, arrived
):
    scalars = [
        pltpu.make_async_copy(plan_ref, plan, arrived.at[0]),
        pltpu.make_async_copy(params_ref, params, arrived.at[1]),
    ]
    fetch = pltpu.make_async_copy(swapped, held, arrived.at[2])
    for copy in (*scalars, fetch):
        copy.start()
    member = lax.axis_index("tensor")
    slot = slot_of(member)
    group = slot // 2

    halves = []
    for core in range(2):
        total = received[core].astype(F32)
        for chip in range(1, CHIPS):
            total = total + received[2 * chip + core].astype(F32)
        halves.append(total)
    lane = lax.broadcasted_iota(jnp.int32, (1, SEQ), 1)
    summed = jnp.concatenate([half.astype(BF16) for half in halves], axis=1)
    ordered = jnp.dot(summed, arrange[...], preferred_element_type=F32)
    zx = ordered[: 2 * CHANNELS, :SEQ]
    bc = ordered[: 2 * CHANNELS, SEQ:]
    steps_raw = ordered[2 * CHANNELS :, :SEQ]

    def columns_of(chunks):
        filler = jnp.zeros((128 - 4 * len(chunks), 128), F32)
        return jnp.concatenate(chunks + [filler], axis=0).T

    state_taps = columns_of(
        [
            taps_ref[:, pl.ds(pl.multiple_of(base + group * STATE, 128), 128)]
            for base in (INNER, INNER + WIDTH_BC)
        ]
    )

    def conv(values, taps):
        total = taps[:, 3:4] * values
        for tap in range(3):
            shift = 3 - tap
            moved = jnp.where(lane >= shift, pltpu.roll(values, shift, 1), 0.0)
            total = total + taps[:, tap : tap + 1] * moved
        return silu(total).astype(BF16)

    b_values = conv(bc[:CHANNELS], state_taps[:, :4])
    c_values = conv(bc[CHANNELS:], state_taps[:, 4:8])
    scores = lax.dot_general(
        b_values.astype(F32).T.astype(BF16), c_values, (((1,), (0,)), ((), ())),
        preferred_element_type=F32,
    )
    gate = silu(zx[:CHANNELS])

    for copy in scalars:
        copy.wait()
    heads = [plan[ORDER + slot * LOCAL + r] for r in range(LOCAL)]
    taps_scratch[...] = columns_of(
        [taps_ref[:, pl.ds(pl.multiple_of((head // 4) * 128, 128), 128)] for head in heads]
    )
    x_taps = jnp.concatenate(
        [
            taps_scratch[pl.ds(pl.multiple_of((heads[r] % 4) * HEAD_DIM, HEAD_DIM), HEAD_DIM), :][
                :, 4 * r : 4 * r + 4
            ]
            for r in range(LOCAL)
        ],
        axis=0,
    )
    x_values = conv(zx[CHANNELS:], x_taps)

    row = lax.broadcasted_iota(jnp.int32, (2 * LOCAL, SEQ), 0)

    def per_head(number):
        values = jnp.zeros((2 * LOCAL, SEQ), F32)
        for r in range(LOCAL):
            values = jnp.where(row == r, params[number, heads[r]], values)
        return values

    raw = steps_raw[: 2 * LOCAL] + per_head(0)
    steps = jnp.maximum(raw, 0.0) + jnp.log1p(jnp.exp(-jnp.abs(raw)))
    rates = -steps * jnp.exp(per_head(1))
    high = rates.astype(BF16)
    rest = rates - high.astype(F32)
    middle = rest.astype(BF16)
    low = (rest - middle.astype(F32)).astype(BF16)
    source = lax.broadcasted_iota(jnp.int32, (SEQ, SEQ), 0)
    target = lax.broadcasted_iota(jnp.int32, (SEQ, SEQ), 1)
    causal = source <= target
    until = jnp.where(causal, 1.0, 0.0).astype(BF16)
    parts = jnp.dot(jnp.concatenate([high, middle, low, low], axis=0), until, preferred_element_type=F32)
    running = parts[:8] + parts[8:16] + parts[16:24]
    columns = jnp.concatenate(
        [running[:LOCAL], steps[:LOCAL], jnp.zeros((128 - 2 * LOCAL, SEQ), F32)], axis=0
    ).T

    mixed = []
    for r in range(LOCAL):
        spread = running[r : r + 1] - columns[:, r : r + 1]
        decay = jnp.exp(jnp.where(causal, spread, -1e30))
        weights = (decay * scores * columns[:, LOCAL + r : LOCAL + r + 1]).astype(BF16)
        x_head = x_values[r * HEAD_DIM : (r + 1) * HEAD_DIM]
        y_head = jnp.dot(x_head, weights, preferred_element_type=F32)
        mixed.append(y_head + params[2, heads[r]] * x_head.astype(F32))
    gated = jnp.concatenate(mixed, axis=0) * gate
    result = gated.T.astype(BF16)
    for index in range(CHIPS):
        out[index] = result
    fetch.wait()


def finish_kernel(plan_ref, gathered, own, peer, out, plan, arrived):
    fetch = pltpu.make_async_copy(plan_ref, plan, arrived)
    fetch.start()
    core = lax.axis_index("tensor") % 2
    normed = []
    for row in range(4):
        values = jnp.concatenate([gathered[2 * row], gathered[2 * row + 1]], axis=1).astype(F32)
        mean_square = jnp.sum(values * values, axis=1, keepdims=True) / (PER_GROUP * HEAD_DIM)
        normed.append((values * lax.rsqrt(mean_square + epsilon)).astype(BF16))
    normed = jnp.concatenate(normed, axis=1)
    fetch.wait()
    begins = [
        plan[ORDER + (2 * row + core) * PER_GROUP + offset] * HEAD_DIM
        for row in range(4)
        for offset in range(PER_GROUP)
    ]

    def columns(ref, place):
        rows = [ref[pl.ds(pl.multiple_of(begin, HEAD_DIM), HEAD_DIM), :] for begin in begins]
        product = jnp.dot(normed, jnp.concatenate(rows, axis=0), preferred_element_type=F32)
        out[:, :, pl.ds(pl.multiple_of(place * ROWS, ROWS), ROWS)] = product.astype(BF16).reshape(
            MEMBERS, SEQ // MEMBERS, ROWS
        )

    columns(own, core)
    columns(peer, 1 - core)


def combine_kernel(received, out):
    for chip in range(CHIPS):
        total = received[2 * chip].astype(F32) + received[2 * chip + 1].astype(F32)
        out[:, 2 * chip * ROWS : (2 * chip + 2) * ROWS] = total.astype(BF16)


SMEM = pl.BlockSpec(memory_space=pltpu.SMEM)
VMEM = pl.BlockSpec(memory_space=pltpu.VMEM)
ANY = pl.BlockSpec(memory_space=pl.ANY)


def shards(hidden, in_weight, out_weight, conv_weight, head_params, packing, head_group):
    own = in_weight.T
    peer = lax.ppermute(own, "tensor", CORE_SWAP)
    per_chip = hidden.reshape(SEQ // MEMBERS, CHIPS, 2 * ROWS).transpose(1, 0, 2)
    acts = lax.all_to_all(
        per_chip, "tensor", split_axis=0, concat_axis=0, tiled=True, axis_index_groups=CHIP_GROUPS
    ).reshape(HALF, 2 * ROWS)

    arrange = pl.pallas_call(
        arrange_kernel,
        out_shape=jax.ShapeDtypeStruct((2 * SEQ, 2 * SEQ), BF16),
        out_specs=VMEM,
        compiler_params=pltpu.CompilerParams(vmem_limit_bytes=2 * 1024 * 1024),
        cost_estimate=pl.CostEstimate(flops=12 * 10**9, bytes_accessed=4 * 10**6, transcendentals=0),
        name="arrange",
    )()
    swapped = lax.ppermute(out_weight, "tensor", CORE_SWAP)

    partial, plan = pl.pallas_call(
        project_kernel,
        out_shape=(
            jax.ShapeDtypeStruct((MEMBERS, PACKED, SEQ), BF16),
            jax.ShapeDtypeStruct((80,), jnp.int32),
        ),
        in_specs=[SMEM, SMEM, VMEM, VMEM, VMEM, pl.BlockSpec(memory_space=pl.ANY)],
        out_specs=(VMEM, SMEM),
        scratch_shapes=[pltpu.VMEM((HEADS, SEQ), F32), pltpu.VMEM((MEMBERS * DT_ROWS, SEQ), F32)],
        compiler_params=pltpu.CompilerParams(vmem_limit_bytes=16 * 1024 * 1024),
        name="project",
    )(packing, head_group, acts, own, peer, arrange)
    partial, swapped = lax.optimization_barrier((partial, swapped))
    received = lax.all_to_all(partial, "tensor", split_axis=0, concat_axis=0, tiled=True)

    gated, held = pl.pallas_call(
        mix_kernel,
        out_shape=(
            jax.ShapeDtypeStruct((CHIPS, SEQ, CHANNELS), BF16),
            jax.ShapeDtypeStruct((INNER, ROWS), BF16),
        ),
        in_specs=[ANY, ANY, VMEM, VMEM, VMEM, ANY],
        out_specs=(VMEM, VMEM),
        scratch_shapes=[
            pltpu.VMEM((128, 128), F32),
            pltpu.SMEM((80,), jnp.int32),
            pltpu.SMEM((3, HEADS), F32),
            pltpu.SemaphoreType.DMA((3,)),
        ],
        compiler_params=pltpu.CompilerParams(vmem_limit_bytes=8 * 1024 * 1024),
        name="mix",
    )(plan, head_params, received, conv_weight, arrange, swapped)
    gathered = lax.all_to_all(
        gated, "tensor", split_axis=0, concat_axis=0, tiled=True, axis_index_groups=CHIP_GROUPS
    )

    share = pl.pallas_call(
        finish_kernel,
        out_shape=jax.ShapeDtypeStruct((MEMBERS, SEQ // MEMBERS, 2 * ROWS), BF16),
        in_specs=[ANY, VMEM, VMEM, VMEM],
        out_specs=VMEM,
        scratch_shapes=[pltpu.SMEM((80,), jnp.int32), pltpu.SemaphoreType.DMA(())],
        compiler_params=pltpu.CompilerParams(vmem_limit_bytes=8 * 1024 * 1024),
        name="finish",
    )(plan, gathered, out_weight, held)
    pieces = lax.all_to_all(share, "tensor", split_axis=0, concat_axis=0, tiled=True)
    return pl.pallas_call(
        combine_kernel,
        out_shape=jax.ShapeDtypeStruct((SEQ // MEMBERS, D), BF16),
        in_specs=[VMEM],
        out_specs=VMEM,
        compiler_params=pltpu.CompilerParams(vmem_limit_bytes=4 * 1024 * 1024),
        name="combine",
    )(pieces)


def solution(mesh):
    in_specs = (P(("dp", "tensor"), None), P("tensor", None), P(None, "tensor"), P(), P(), P(), P())
    out_specs = P(("dp", "tensor"), None)
    return jax.shard_map(shards, mesh=mesh, in_specs=in_specs, out_specs=out_specs, check_vma=False)
```

```python
import functools

import jax
import jax.numpy as jnp
from jax import lax
from jax.experimental import pallas as pl
from jax.experimental.pallas import tpu as pltpu
from jax.sharding import PartitionSpec as P

D = 4096
HEADS = 64
HEAD_DIM = 32
GROUPS = 8
STATE = 128
SEQ = 128
INNER = HEADS * HEAD_DIM
WIDTH_BC = GROUPS * STATE
COLS = 2 * INNER + 2 * WIDTH_BC + HEADS
MEMBERS = 16
CHIPS = MEMBERS // 2
ROWS = D // MEMBERS
HALF = SEQ // 2
PER_GROUP = HEADS // GROUPS
LOCAL = HEADS // MEMBERS
CHANNELS = LOCAL * HEAD_DIM
DT_ROWS = 16
PACKED = 2 * CHANNELS + DT_ROWS

epsilon = 1e-05
F32 = jnp.float32
BF16 = jnp.bfloat16

NT = (((1,), (1,)), ((), ()))


CORE_SWAP = [(member, member ^ 1) for member in range(MEMBERS)]
CHIP_GROUPS = [[2 * chip + core for chip in range(CHIPS)] for core in range(2)]
ORDER, STARTS = 0, HEADS


def arrange_kernel(arrange):
    source = lax.broadcasted_iota(jnp.int32, (2 * SEQ, 2 * SEQ), 0)
    target = lax.broadcasted_iota(jnp.int32, (2 * SEQ, 2 * SEQ), 1)
    column = source % HALF
    token = 16 * (column // 8) + 8 * (source // SEQ) + column % 8
    wanted = token + SEQ * ((source // HALF) % 2)
    arrange[...] = jnp.where(wanted == target, 1.0, 0.0).astype(BF16)


def slot_of(member):
    return (2 * (member // 4) + member % 2) * 2 + (member // 2) % 2


def project_kernel(packing, head_group, acts, own, peer, _, out, plan, steps_ref, sorted_ref):
    begin = jnp.int32(0)
    for place in range(5):
        number = packing[place]
        plan[STARTS + number] = begin
        begin = begin + jnp.where(number < 2, INNER, jnp.where(number < 4, WIDTH_BC, HEADS))
    for spare in range(STARTS + 5, 80):
        plan[spare] = 0
    filled = jnp.int32(0)
    for head in range(HEADS):
        group = head_group[head]
        position = lax.shift_right_logical(filled, 4 * group) & 15
        plan[ORDER + group * PER_GROUP + position] = head
        filled = filled + lax.shift_left(jnp.int32(1), 4 * group)

    rows = acts[...]
    is_first = lax.axis_index("tensor") % 2 == 0
    first, second = rows[:, :ROWS], rows[:, ROWS:]
    both = jnp.concatenate(
        [jnp.where(is_first, first, second), jnp.where(is_first, second, first)], axis=1
    )
    both = jnp.concatenate([both, both], axis=0).astype(F32).T.astype(BF16)
    low = lax.broadcasted_iota(jnp.int32, (CHANNELS, SEQ), 1) < HALF

    def taken(number, begin, extent):
        where = pl.ds(pl.multiple_of(plan[STARTS + number] + begin, HEAD_DIM), extent)
        return jnp.concatenate([own[where, :], peer[where, :]], axis=1)

    for group in range(GROUPS):
        heads = [plan[ORDER + group * PER_GROUP + offset] for offset in range(PER_GROUP)]
        weights = jnp.concatenate(
            [taken(number, head * HEAD_DIM, HEAD_DIM) for number in range(2) for head in heads]
            + [taken(number, group * STATE, STATE) for number in range(2, 4)],
            axis=0,
        )
        parts = jnp.dot(weights, both, preferred_element_type=F32)
        for side in range(2):
            target = 4 * (group // 2) + 2 * side + group % 2
            for number in range(2):
                begin = (2 * number + side) * CHANNELS
                other = (4 + number) * CHANNELS
                out[target, number * CHANNELS : (number + 1) * CHANNELS, :] = jnp.where(
                    low, parts[begin : begin + CHANNELS], parts[other : other + CHANNELS]
                ).astype(BF16)

    steps_ref[...] = jnp.dot(taken(4, 0, HEADS), both, preferred_element_type=F32)
    sorted_ref[...] = jnp.zeros_like(sorted_ref)
    for member in range(MEMBERS):
        for r in range(LOCAL):
            sorted_ref[pl.ds(member * DT_ROWS + r, 1), :] = steps_ref[
                pl.ds(plan[ORDER + slot_of(member) * LOCAL + r], 1), :
            ]
    out[:, 2 * CHANNELS :, :] = sorted_ref[...].astype(BF16).reshape(MEMBERS, DT_ROWS, SEQ)


def silu(values):
    return values / (1.0 + jnp.exp(-values))


def mix_kernel(
    plan_ref, params_ref, received, taps_ref, arrange, weight, swapped,
    out, mine, theirs, taps_scratch, held, plan, params, arrived,
):
    scalars = [
        pltpu.make_async_copy(plan_ref, plan, arrived.at[0]),
        pltpu.make_async_copy(params_ref, params, arrived.at[1]),
    ]
    fetch = pltpu.make_async_copy(swapped, held, arrived.at[2])
    for copy in (*scalars, fetch):
        copy.start()
    member = lax.axis_index("tensor")
    slot = slot_of(member)
    group = slot // 2

    halves = []
    for core in range(2):
        total = received[core].astype(F32)
        for chip in range(1, CHIPS):
            total = total + received[2 * chip + core].astype(F32)
        halves.append(total)
    lane = lax.broadcasted_iota(jnp.int32, (1, SEQ), 1)
    summed = jnp.concatenate([half.astype(BF16) for half in halves], axis=1)
    ordered = jnp.dot(summed, arrange[...], preferred_element_type=F32)
    zx = ordered[: 2 * CHANNELS, :SEQ]
    bc = ordered[: 2 * CHANNELS, SEQ:]
    steps_raw = ordered[2 * CHANNELS :, :SEQ]

    def columns_of(chunks):
        filler = jnp.zeros((128 - 4 * len(chunks), 128), F32)
        return jnp.concatenate(chunks + [filler], axis=0).T

    state_taps = columns_of(
        [
            taps_ref[:, pl.ds(pl.multiple_of(base + group * STATE, 128), 128)]
            for base in (INNER, INNER + WIDTH_BC)
        ]
    )

    def conv(values, taps):
        total = taps[:, 3:4] * values
        for tap in range(3):
            shift = 3 - tap
            moved = jnp.where(lane >= shift, pltpu.roll(values, shift, 1), 0.0)
            total = total + taps[:, tap : tap + 1] * moved
        return silu(total).astype(BF16)

    b_values = conv(bc[:CHANNELS], state_taps[:, :4])
    c_values = conv(bc[CHANNELS:], state_taps[:, 4:8])
    scores = lax.dot_general(
        b_values.astype(F32).T.astype(BF16), c_values, (((1,), (0,)), ((), ())),
        preferred_element_type=F32,
    )
    gate = silu(zx[:CHANNELS])

    for copy in scalars:
        copy.wait()
    heads = [plan[ORDER + slot * LOCAL + r] for r in range(LOCAL)]
    taps_scratch[...] = columns_of(
        [taps_ref[:, pl.ds(pl.multiple_of((head // 4) * 128, 128), 128)] for head in heads]
    )
    x_taps = jnp.concatenate(
        [
            taps_scratch[pl.ds(pl.multiple_of((heads[r] % 4) * HEAD_DIM, HEAD_DIM), HEAD_DIM), :][
                :, 4 * r : 4 * r + 4
            ]
            for r in range(LOCAL)
        ],
        axis=0,
    )
    x_values = conv(zx[CHANNELS:], x_taps)

    row = lax.broadcasted_iota(jnp.int32, (2 * LOCAL, SEQ), 0)

    def per_head(number):
        values = jnp.zeros((2 * LOCAL, SEQ), F32)
        for r in range(LOCAL):
            values = jnp.where(row == r, params[number, heads[r]], values)
        return values

    raw = steps_raw[: 2 * LOCAL] + per_head(0)
    steps = jnp.maximum(raw, 0.0) + jnp.log1p(jnp.exp(-jnp.abs(raw)))
    rates = -steps * jnp.exp(per_head(1))
    high = rates.astype(BF16)
    rest = rates - high.astype(F32)
    middle = rest.astype(BF16)
    low = (rest - middle.astype(F32)).astype(BF16)
    source = lax.broadcasted_iota(jnp.int32, (SEQ, SEQ), 0)
    target = lax.broadcasted_iota(jnp.int32, (SEQ, SEQ), 1)
    causal = source <= target
    until = jnp.where(causal, 1.0, 0.0).astype(BF16)
    parts = jnp.dot(jnp.concatenate([high, middle, low, low], axis=0), until, preferred_element_type=F32)
    running = parts[:8] + parts[8:16] + parts[16:24]
    columns = jnp.concatenate(
        [running[:LOCAL], steps[:LOCAL], jnp.zeros((128 - 2 * LOCAL, SEQ), F32)], axis=0
    ).T

    mixed = []
    for r in range(LOCAL):
        spread = running[r : r + 1] - columns[:, r : r + 1]
        decay = jnp.exp(jnp.where(causal, spread, -1e30))
        weights = (decay * scores * columns[:, LOCAL + r : LOCAL + r + 1]).astype(BF16)
        x_head = x_values[r * HEAD_DIM : (r + 1) * HEAD_DIM]
        y_head = jnp.dot(x_head, weights, preferred_element_type=F32)
        mixed.append(y_head + params[2, heads[r]] * x_head.astype(F32))
    gated = jnp.concatenate(mixed, axis=0) * gate
    result = gated.T.astype(BF16)
    for index in range(CHIPS):
        out[index] = result
    begins = [
        plan[ORDER + (2 * row + member % 2) * PER_GROUP + offset] * HEAD_DIM
        for row in range(4)
        for offset in range(PER_GROUP)
    ]

    def sort_rows(source, sink):
        for place, begin in enumerate(begins):
            sink[place * HEAD_DIM : (place + 1) * HEAD_DIM, :] = source[
                pl.ds(pl.multiple_of(begin, HEAD_DIM), HEAD_DIM), :
            ]

    sort_rows(weight, mine)
    fetch.wait()
    sort_rows(held, theirs)


def finish_kernel(gathered, own, peer, out):
    core = lax.axis_index("tensor") % 2
    normed = []
    for row in range(4):
        values = jnp.concatenate([gathered[2 * row], gathered[2 * row + 1]], axis=1).astype(F32)
        mean_square = jnp.sum(values * values, axis=1, keepdims=True) / (PER_GROUP * HEAD_DIM)
        normed.append((values * lax.rsqrt(mean_square + epsilon)).astype(BF16))
    normed = jnp.concatenate(normed, axis=1)
    for ref, place in ((own, core), (peer, 1 - core)):
        product = jnp.dot(normed, ref[...], preferred_element_type=F32)
        out[:, :, pl.ds(pl.multiple_of(place * ROWS, ROWS), ROWS)] = product.astype(BF16).reshape(
            MEMBERS, SEQ // MEMBERS, ROWS
        )


def combine_kernel(received, out):
    for chip in range(CHIPS):
        total = received[2 * chip].astype(F32) + received[2 * chip + 1].astype(F32)
        out[:, 2 * chip * ROWS : (2 * chip + 2) * ROWS] = total.astype(BF16)


SMEM = pl.BlockSpec(memory_space=pltpu.SMEM)
VMEM = pl.BlockSpec(memory_space=pltpu.VMEM)
ANY = pl.BlockSpec(memory_space=pl.ANY)


def shards(hidden, in_weight, out_weight, conv_weight, head_params, packing, head_group):
    own = in_weight.T
    peer = lax.ppermute(own, "tensor", CORE_SWAP)
    per_chip = hidden.reshape(SEQ // MEMBERS, CHIPS, 2 * ROWS).transpose(1, 0, 2)
    acts = lax.all_to_all(
        per_chip, "tensor", split_axis=0, concat_axis=0, tiled=True, axis_index_groups=CHIP_GROUPS
    ).reshape(HALF, 2 * ROWS)

    arrange = pl.pallas_call(
        arrange_kernel,
        out_shape=jax.ShapeDtypeStruct((2 * SEQ, 2 * SEQ), BF16),
        out_specs=VMEM,
        compiler_params=pltpu.CompilerParams(vmem_limit_bytes=2 * 1024 * 1024),
        cost_estimate=pl.CostEstimate(flops=12 * 10**9, bytes_accessed=4 * 10**6, transcendentals=0),
        name="arrange",
    )()
    swapped = lax.ppermute(out_weight, "tensor", CORE_SWAP)

    partial, plan = pl.pallas_call(
        project_kernel,
        out_shape=(
            jax.ShapeDtypeStruct((MEMBERS, PACKED, SEQ), BF16),
            jax.ShapeDtypeStruct((80,), jnp.int32),
        ),
        in_specs=[SMEM, SMEM, VMEM, VMEM, VMEM, pl.BlockSpec(memory_space=pl.ANY)],
        out_specs=(VMEM, SMEM),
        scratch_shapes=[pltpu.VMEM((HEADS, SEQ), F32), pltpu.VMEM((MEMBERS * DT_ROWS, SEQ), F32)],
        compiler_params=pltpu.CompilerParams(vmem_limit_bytes=16 * 1024 * 1024),
        name="project",
    )(packing, head_group, acts, own, peer, arrange)
    partial, swapped = lax.optimization_barrier((partial, swapped))
    received = lax.all_to_all(partial, "tensor", split_axis=0, concat_axis=0, tiled=True)

    gated, mine, theirs = pl.pallas_call(
        mix_kernel,
        out_shape=(
            jax.ShapeDtypeStruct((CHIPS, SEQ, CHANNELS), BF16),
            jax.ShapeDtypeStruct((INNER // 2, ROWS), BF16),
            jax.ShapeDtypeStruct((INNER // 2, ROWS), BF16),
        ),
        in_specs=[ANY, ANY, VMEM, VMEM, VMEM, VMEM, ANY],
        out_specs=(VMEM, VMEM, VMEM),
        scratch_shapes=[
            pltpu.VMEM((128, 128), F32),
            pltpu.VMEM((INNER, ROWS), BF16),
            pltpu.SMEM((80,), jnp.int32),
            pltpu.SMEM((3, HEADS), F32),
            pltpu.SemaphoreType.DMA((3,)),
        ],
        compiler_params=pltpu.CompilerParams(vmem_limit_bytes=8 * 1024 * 1024),
        name="mix",
    )(plan, head_params, received, conv_weight, arrange, out_weight, swapped)
    gathered = lax.all_to_all(
        gated, "tensor", split_axis=0, concat_axis=0, tiled=True, axis_index_groups=CHIP_GROUPS
    )

    share = pl.pallas_call(
        finish_kernel,
        out_shape=jax.ShapeDtypeStruct((MEMBERS, SEQ // MEMBERS, 2 * ROWS), BF16),
        in_specs=[VMEM, VMEM, VMEM],
        out_specs=VMEM,
        compiler_params=pltpu.CompilerParams(vmem_limit_bytes=8 * 1024 * 1024),
        name="finish",
    )(gathered, mine, theirs)
    pieces = lax.all_to_all(share, "tensor", split_axis=0, concat_axis=0, tiled=True)
    return pl.pallas_call(
        combine_kernel,
        out_shape=jax.ShapeDtypeStruct((SEQ // MEMBERS, D), BF16),
        in_specs=[VMEM],
        out_specs=VMEM,
        compiler_params=pltpu.CompilerParams(vmem_limit_bytes=4 * 1024 * 1024),
        name="combine",
    )(pieces)


def solution(mesh):
    in_specs = (P(("dp", "tensor"), None), P("tensor", None), P(None, "tensor"), P(), P(), P(), P())
    out_specs = P(("dp", "tensor"), None)
    return jax.shard_map(shards, mesh=mesh, in_specs=in_specs, out_specs=out_specs, check_vma=False)
```

```python
import functools

import jax
import jax.numpy as jnp
from jax import lax
from jax.experimental import pallas as pl
from jax.experimental.pallas import tpu as pltpu
from jax.sharding import PartitionSpec as P

D = 4096
HEADS = 64
HEAD_DIM = 32
GROUPS = 8
STATE = 128
SEQ = 128
INNER = HEADS * HEAD_DIM
WIDTH_BC = GROUPS * STATE
COLS = 2 * INNER + 2 * WIDTH_BC + HEADS
MEMBERS = 16
CHIPS = MEMBERS // 2
ROWS = D // MEMBERS
HALF = SEQ // 2
PER_GROUP = HEADS // GROUPS
LOCAL = HEADS // MEMBERS
CHANNELS = LOCAL * HEAD_DIM
DT_ROWS = 16
PACKED = 2 * CHANNELS + DT_ROWS

epsilon = 1e-05
F32 = jnp.float32
BF16 = jnp.bfloat16

NT = (((1,), (1,)), ((), ()))


CORE_SWAP = [(member, member ^ 1) for member in range(MEMBERS)]
CHIP_GROUPS = [[2 * chip + core for chip in range(CHIPS)] for core in range(2)]
ORDER, STARTS = 0, HEADS
STREAMS = tuple((begin, min(1600, COLS - begin)) for begin in range(0, COLS, 1600))


def arrange_kernel(arrange):
    source = lax.broadcasted_iota(jnp.int32, (2 * SEQ, 2 * SEQ), 0)
    target = lax.broadcasted_iota(jnp.int32, (2 * SEQ, 2 * SEQ), 1)
    column = source % HALF
    token = 16 * (column // 8) + 8 * (source // SEQ) + column % 8
    wanted = token + SEQ * ((source // HALF) % 2)
    arrange[...] = jnp.where(wanted == target, 1.0, 0.0).astype(BF16)


def slot_of(member):
    return (2 * (member // 4) + member % 2) * 2 + (member // 2) % 2


def project_kernel(
    packing_ref, group_ref, acts, own, peer_ref, _, out, plan,
    steps_ref, sorted_ref, peer, packing, head_group, arrived,
):
    scalars = [
        pltpu.make_async_copy(packing_ref, packing, arrived.at[0]),
        pltpu.make_async_copy(group_ref, head_group, arrived.at[1]),
    ]
    streams = [
        pltpu.make_async_copy(
            peer_ref.at[pl.ds(begin, extent), :], peer.at[pl.ds(begin, extent), :], arrived.at[2 + index]
        )
        for index, (begin, extent) in enumerate(STREAMS)
    ]
    for copy in (*scalars, *streams):
        copy.start()
    for copy in scalars:
        copy.wait()
    begin = jnp.int32(0)
    for place in range(5):
        number = packing[place]
        plan[STARTS + number] = begin
        begin = begin + jnp.where(number < 2, INNER, jnp.where(number < 4, WIDTH_BC, HEADS))
    for spare in range(STARTS + 5, 80):
        plan[spare] = 0
    filled = jnp.int32(0)
    for head in range(HEADS):
        group = head_group[head]
        position = lax.shift_right_logical(filled, 4 * group) & 15
        plan[ORDER + group * PER_GROUP + position] = head
        filled = filled + lax.shift_left(jnp.int32(1), 4 * group)

    rows = acts[...]
    is_first = lax.axis_index("tensor") % 2 == 0
    first, second = rows[:, :ROWS], rows[:, ROWS:]
    both = jnp.concatenate(
        [jnp.where(is_first, first, second), jnp.where(is_first, second, first)], axis=1
    )
    both = jnp.concatenate([both, both], axis=0).astype(F32).T.astype(BF16)
    low = lax.broadcasted_iota(jnp.int32, (CHANNELS, SEQ), 1) < HALF
    for copy in streams:
        copy.wait()

    def taken(number, begin, extent):
        where = pl.ds(pl.multiple_of(plan[STARTS + number] + begin, HEAD_DIM), extent)
        return jnp.concatenate([own[where, :], peer[where, :]], axis=1)

    for group in range(GROUPS):
        heads = [plan[ORDER + group * PER_GROUP + offset] for offset in range(PER_GROUP)]
        weights = jnp.concatenate(
            [taken(number, head * HEAD_DIM, HEAD_DIM) for number in range(2) for head in heads]
            + [taken(number, group * STATE, STATE) for number in range(2, 4)],
            axis=0,
        )
        parts = jnp.dot(weights, both, preferred_element_type=F32)
        for side in range(2):
            target = 4 * (group // 2) + 2 * side + group % 2
            for number in range(2):
                begin = (2 * number + side) * CHANNELS
                other = (4 + number) * CHANNELS
                out[target, number * CHANNELS : (number + 1) * CHANNELS, :] = jnp.where(
                    low, parts[begin : begin + CHANNELS], parts[other : other + CHANNELS]
                ).astype(BF16)

    steps_ref[...] = jnp.dot(taken(4, 0, HEADS), both, preferred_element_type=F32)
    sorted_ref[...] = jnp.zeros_like(sorted_ref)
    for member in range(MEMBERS):
        for r in range(LOCAL):
            sorted_ref[pl.ds(member * DT_ROWS + r, 1), :] = steps_ref[
                pl.ds(plan[ORDER + slot_of(member) * LOCAL + r], 1), :
            ]
    out[:, 2 * CHANNELS :, :] = sorted_ref[...].astype(BF16).reshape(MEMBERS, DT_ROWS, SEQ)


def silu(values):
    return values / (1.0 + jnp.exp(-values))


def mix_kernel(
    plan_ref, params_ref, received, taps_ref, arrange, weight, swapped,
    out, mine, theirs, taps_scratch, held, plan, params, arrived,
):
    scalars = [
        pltpu.make_async_copy(plan_ref, plan, arrived.at[0]),
        pltpu.make_async_copy(params_ref, params, arrived.at[1]),
    ]
    fetch = pltpu.make_async_copy(swapped, held, arrived.at[2])
    for copy in (*scalars, fetch):
        copy.start()
    member = lax.axis_index("tensor")
    slot = slot_of(member)
    group = slot // 2

    halves = []
    for core in range(2):
        total = received[core].astype(F32)
        for chip in range(1, CHIPS):
            total = total + received[2 * chip + core].astype(F32)
        halves.append(total)
    lane = lax.broadcasted_iota(jnp.int32, (1, SEQ), 1)
    summed = jnp.concatenate([half.astype(BF16) for half in halves], axis=1)
    ordered = jnp.dot(summed, arrange[...], preferred_element_type=F32)
    zx = ordered[: 2 * CHANNELS, :SEQ]
    bc = ordered[: 2 * CHANNELS, SEQ:]
    steps_raw = ordered[2 * CHANNELS :, :SEQ]

    def columns_of(chunks):
        filler = jnp.zeros((128 - 4 * len(chunks), 128), F32)
        return jnp.concatenate(chunks + [filler], axis=0).T

    state_taps = columns_of(
        [
            taps_ref[:, pl.ds(pl.multiple_of(base + group * STATE, 128), 128)]
            for base in (INNER, INNER + WIDTH_BC)
        ]
    )

    def conv(values, taps):
        total = taps[:, 3:4] * values
        for tap in range(3):
            shift = 3 - tap
            moved = jnp.where(lane >= shift, pltpu.roll(values, shift, 1), 0.0)
            total = total + taps[:, tap : tap + 1] * moved
        return silu(total).astype(BF16)

    b_values = conv(bc[:CHANNELS], state_taps[:, :4])
    c_values = conv(bc[CHANNELS:], state_taps[:, 4:8])
    scores = lax.dot_general(
        b_values.astype(F32).T.astype(BF16), c_values, (((1,), (0,)), ((), ())),
        preferred_element_type=F32,
    )
    gate = silu(zx[:CHANNELS])

    for copy in scalars:
        copy.wait()
    heads = [plan[ORDER + slot * LOCAL + r] for r in range(LOCAL)]
    taps_scratch[...] = columns_of(
        [taps_ref[:, pl.ds(pl.multiple_of((head // 4) * 128, 128), 128)] for head in heads]
    )
    x_taps = jnp.concatenate(
        [
            taps_scratch[pl.ds(pl.multiple_of((heads[r] % 4) * HEAD_DIM, HEAD_DIM), HEAD_DIM), :][
                :, 4 * r : 4 * r + 4
            ]
            for r in range(LOCAL)
        ],
        axis=0,
    )
    x_values = conv(zx[CHANNELS:], x_taps)

    row = lax.broadcasted_iota(jnp.int32, (2 * LOCAL, SEQ), 0)

    def per_head(number):
        values = jnp.zeros((2 * LOCAL, SEQ), F32)
        for r in range(LOCAL):
            values = jnp.where(row == r, params[number, heads[r]], values)
        return values

    raw = steps_raw[: 2 * LOCAL] + per_head(0)
    steps = jnp.maximum(raw, 0.0) + jnp.log1p(jnp.exp(-jnp.abs(raw)))
    rates = -steps * jnp.exp(per_head(1))
    high = rates.astype(BF16)
    rest = rates - high.astype(F32)
    middle = rest.astype(BF16)
    low = (rest - middle.astype(F32)).astype(BF16)
    source = lax.broadcasted_iota(jnp.int32, (SEQ, SEQ), 0)
    target = lax.broadcasted_iota(jnp.int32, (SEQ, SEQ), 1)
    causal = source <= target
    until = jnp.where(causal, 1.0, 0.0).astype(BF16)
    parts = jnp.dot(jnp.concatenate([high, middle, low, low], axis=0), until, preferred_element_type=F32)
    running = parts[:8] + parts[8:16] + parts[16:24]
    columns = jnp.concatenate(
        [running[:LOCAL], steps[:LOCAL], jnp.zeros((128 - 2 * LOCAL, SEQ), F32)], axis=0
    ).T

    mixed = []
    for r in range(LOCAL):
        spread = running[r : r + 1] - columns[:, r : r + 1]
        decay = jnp.exp(jnp.where(causal, spread, -1e30))
        weights = (decay * scores * columns[:, LOCAL + r : LOCAL + r + 1]).astype(BF16)
        x_head = x_values[r * HEAD_DIM : (r + 1) * HEAD_DIM]
        y_head = jnp.dot(x_head, weights, preferred_element_type=F32)
        mixed.append(y_head + params[2, heads[r]] * x_head.astype(F32))
    gated = jnp.concatenate(mixed, axis=0) * gate
    result = gated.T.astype(BF16)
    for index in range(CHIPS):
        out[index] = result
    begins = [
        plan[ORDER + (2 * row + member % 2) * PER_GROUP + offset] * HEAD_DIM
        for row in range(4)
        for offset in range(PER_GROUP)
    ]

    def sort_rows(source, sink):
        for place, begin in enumerate(begins):
            sink[place * HEAD_DIM : (place + 1) * HEAD_DIM, :] = source[
                pl.ds(pl.multiple_of(begin, HEAD_DIM), HEAD_DIM), :
            ]

    sort_rows(weight, mine)
    fetch.wait()
    sort_rows(held, theirs)


def finish_kernel(gathered, own, peer, out):
    core = lax.axis_index("tensor") % 2
    normed = []
    for row in range(4):
        values = jnp.concatenate([gathered[2 * row], gathered[2 * row + 1]], axis=1).astype(F32)
        mean_square = jnp.sum(values * values, axis=1, keepdims=True) / (PER_GROUP * HEAD_DIM)
        normed.append((values * lax.rsqrt(mean_square + epsilon)).astype(BF16))
    normed = jnp.concatenate(normed, axis=1)
    for ref, place in ((own, core), (peer, 1 - core)):
        product = jnp.dot(normed, ref[...], preferred_element_type=F32)
        out[:, :, pl.ds(pl.multiple_of(place * ROWS, ROWS), ROWS)] = product.astype(BF16).reshape(
            MEMBERS, SEQ // MEMBERS, ROWS
        )


def combine_kernel(received, out):
    for chip in range(CHIPS):
        total = received[2 * chip].astype(F32) + received[2 * chip + 1].astype(F32)
        out[:, 2 * chip * ROWS : (2 * chip + 2) * ROWS] = total.astype(BF16)


SMEM = pl.BlockSpec(memory_space=pltpu.SMEM)
VMEM = pl.BlockSpec(memory_space=pltpu.VMEM)
ANY = pl.BlockSpec(memory_space=pl.ANY)


def shards(hidden, in_weight, out_weight, conv_weight, head_params, packing, head_group):
    own = in_weight.T
    peer = lax.ppermute(own, "tensor", CORE_SWAP)
    per_chip = hidden.reshape(SEQ // MEMBERS, CHIPS, 2 * ROWS).transpose(1, 0, 2)
    acts = lax.all_to_all(
        per_chip, "tensor", split_axis=0, concat_axis=0, tiled=True, axis_index_groups=CHIP_GROUPS
    ).reshape(HALF, 2 * ROWS)

    arrange = pl.pallas_call(
        arrange_kernel,
        out_shape=jax.ShapeDtypeStruct((2 * SEQ, 2 * SEQ), BF16),
        out_specs=VMEM,
        compiler_params=pltpu.CompilerParams(vmem_limit_bytes=2 * 1024 * 1024),
        cost_estimate=pl.CostEstimate(flops=12 * 10**9, bytes_accessed=4 * 10**6, transcendentals=0),
        name="arrange",
    )()
    swapped = lax.ppermute(out_weight, "tensor", CORE_SWAP)

    partial, plan = pl.pallas_call(
        project_kernel,
        out_shape=(
            jax.ShapeDtypeStruct((MEMBERS, PACKED, SEQ), BF16),
            jax.ShapeDtypeStruct((80,), jnp.int32),
        ),
        in_specs=[ANY, ANY, VMEM, VMEM, ANY, ANY],
        out_specs=(VMEM, SMEM),
        scratch_shapes=[
            pltpu.VMEM((HEADS, SEQ), F32),
            pltpu.VMEM((MEMBERS * DT_ROWS, SEQ), F32),
            pltpu.VMEM((COLS, ROWS), BF16),
            pltpu.SMEM((5,), jnp.int32),
            pltpu.SMEM((HEADS,), jnp.int32),
            pltpu.SemaphoreType.DMA((2 + len(STREAMS),)),
        ],
        compiler_params=pltpu.CompilerParams(vmem_limit_bytes=16 * 1024 * 1024),
        name="project",
    )(packing, head_group, acts, own, peer, arrange)
    partial, swapped = lax.optimization_barrier((partial, swapped))
    received = lax.all_to_all(partial, "tensor", split_axis=0, concat_axis=0, tiled=True)

    gated, mine, theirs = pl.pallas_call(
        mix_kernel,
        out_shape=(
            jax.ShapeDtypeStruct((CHIPS, SEQ, CHANNELS), BF16),
            jax.ShapeDtypeStruct((INNER // 2, ROWS), BF16),
            jax.ShapeDtypeStruct((INNER // 2, ROWS), BF16),
        ),
        in_specs=[ANY, ANY, VMEM, VMEM, VMEM, VMEM, ANY],
        out_specs=(VMEM, VMEM, VMEM),
        scratch_shapes=[
            pltpu.VMEM((128, 128), F32),
            pltpu.VMEM((INNER, ROWS), BF16),
            pltpu.SMEM((80,), jnp.int32),
            pltpu.SMEM((3, HEADS), F32),
            pltpu.SemaphoreType.DMA((3,)),
        ],
        compiler_params=pltpu.CompilerParams(vmem_limit_bytes=8 * 1024 * 1024),
        name="mix",
    )(plan, head_params, received, conv_weight, arrange, out_weight, swapped)
    gathered = lax.all_to_all(
        gated, "tensor", split_axis=0, concat_axis=0, tiled=True, axis_index_groups=CHIP_GROUPS
    )

    share = pl.pallas_call(
        finish_kernel,
        out_shape=jax.ShapeDtypeStruct((MEMBERS, SEQ // MEMBERS, 2 * ROWS), BF16),
        in_specs=[VMEM, VMEM, VMEM],
        out_specs=VMEM,
        compiler_params=pltpu.CompilerParams(vmem_limit_bytes=8 * 1024 * 1024),
        name="finish",
    )(gathered, mine, theirs)
    pieces = lax.all_to_all(share, "tensor", split_axis=0, concat_axis=0, tiled=True)
    return pl.pallas_call(
        combine_kernel,
        out_shape=jax.ShapeDtypeStruct((SEQ // MEMBERS, D), BF16),
        in_specs=[VMEM],
        out_specs=VMEM,
        compiler_params=pltpu.CompilerParams(vmem_limit_bytes=4 * 1024 * 1024),
        name="combine",
    )(pieces)


def solution(mesh):
    in_specs = (P(("dp", "tensor"), None), P("tensor", None), P(None, "tensor"), P(), P(), P(), P())
    out_specs = P(("dp", "tensor"), None)
    return jax.shard_map(shards, mesh=mesh, in_specs=in_specs, out_specs=out_specs, check_vma=False)
```

```python
import functools

import jax
import jax.numpy as jnp
from jax import lax
from jax.experimental import pallas as pl
from jax.experimental.pallas import tpu as pltpu
from jax.sharding import PartitionSpec as P

D = 4096
HEADS = 64
HEAD_DIM = 32
GROUPS = 8
STATE = 128
SEQ = 128
INNER = HEADS * HEAD_DIM
WIDTH_BC = GROUPS * STATE
COLS = 2 * INNER + 2 * WIDTH_BC + HEADS
MEMBERS = 16
CHIPS = MEMBERS // 2
ROWS = D // MEMBERS
HALF = SEQ // 2
PER_GROUP = HEADS // GROUPS
LOCAL = HEADS // MEMBERS
CHANNELS = LOCAL * HEAD_DIM
DT_ROWS = 16
PACKED = 2 * CHANNELS + DT_ROWS

epsilon = 1e-05
F32 = jnp.float32
BF16 = jnp.bfloat16

NT = (((1,), (1,)), ((), ()))


CORE_SWAP = [(member, member ^ 1) for member in range(MEMBERS)]
CHIP_GROUPS = [[2 * chip + core for chip in range(CHIPS)] for core in range(2)]
ORDER, STARTS = 0, HEADS
STREAMS = tuple((begin, min(800, COLS - begin)) for begin in range(0, COLS, 800))


def arrange_kernel(arrange):
    source = lax.broadcasted_iota(jnp.int32, (2 * SEQ, 2 * SEQ), 0)
    target = lax.broadcasted_iota(jnp.int32, (2 * SEQ, 2 * SEQ), 1)
    column = source % HALF
    token = 16 * (column // 8) + 8 * (source // SEQ) + column % 8
    wanted = token + SEQ * ((source // HALF) % 2)
    arrange[...] = jnp.where(wanted == target, 1.0, 0.0).astype(BF16)


def slot_of(member):
    return (2 * (member // 4) + member % 2) * 2 + (member // 2) % 2


def project_kernel(
    packing_ref, group_ref, acts, own, peer_ref, _, out, plan,
    steps_ref, sorted_ref, peer, packing, head_group, arrived,
):
    scalars = [
        pltpu.make_async_copy(packing_ref, packing, arrived.at[0]),
        pltpu.make_async_copy(group_ref, head_group, arrived.at[1]),
    ]
    streams = [
        pltpu.make_async_copy(
            peer_ref.at[pl.ds(begin, extent), :], peer.at[pl.ds(begin, extent), :], arrived.at[2 + index]
        )
        for index, (begin, extent) in enumerate(STREAMS)
    ]
    for copy in (*scalars, *streams):
        copy.start()
    for copy in scalars:
        copy.wait()
    begin = jnp.int32(0)
    for place in range(5):
        number = packing[place]
        plan[STARTS + number] = begin
        begin = begin + jnp.where(number < 2, INNER, jnp.where(number < 4, WIDTH_BC, HEADS))
    for spare in range(STARTS + 5, 80):
        plan[spare] = 0
    filled = jnp.int32(0)
    for head in range(HEADS):
        group = head_group[head]
        position = lax.shift_right_logical(filled, 4 * group) & 15
        plan[ORDER + group * PER_GROUP + position] = head
        filled = filled + lax.shift_left(jnp.int32(1), 4 * group)

    rows = acts[...]
    is_first = lax.axis_index("tensor") % 2 == 0
    first, second = rows[:, :ROWS], rows[:, ROWS:]
    both = jnp.concatenate(
        [jnp.where(is_first, first, second), jnp.where(is_first, second, first)], axis=1
    )
    both = jnp.concatenate([both, both], axis=0).astype(F32).T.astype(BF16)
    low = lax.broadcasted_iota(jnp.int32, (CHANNELS, SEQ), 1) < HALF
    for copy in streams:
        copy.wait()

    def taken(number, begin, extent):
        where = pl.ds(pl.multiple_of(plan[STARTS + number] + begin, HEAD_DIM), extent)
        return jnp.concatenate([own[where, :], peer[where, :]], axis=1)

    for group in range(GROUPS):
        heads = [plan[ORDER + group * PER_GROUP + offset] for offset in range(PER_GROUP)]
        weights = jnp.concatenate(
            [taken(number, head * HEAD_DIM, HEAD_DIM) for number in range(2) for head in heads]
            + [taken(number, group * STATE, STATE) for number in range(2, 4)],
            axis=0,
        )
        parts = jnp.dot(weights, both, preferred_element_type=F32)
        for side in range(2):
            target = 4 * (group // 2) + 2 * side + group % 2
            for number in range(2):
                begin = (2 * number + side) * CHANNELS
                other = (4 + number) * CHANNELS
                out[target, number * CHANNELS : (number + 1) * CHANNELS, :] = jnp.where(
                    low, parts[begin : begin + CHANNELS], parts[other : other + CHANNELS]
                ).astype(BF16)

    steps_ref[...] = jnp.dot(taken(4, 0, HEADS), both, preferred_element_type=F32)
    sorted_ref[...] = jnp.zeros_like(sorted_ref)
    for member in range(MEMBERS):
        for r in range(LOCAL):
            sorted_ref[pl.ds(member * DT_ROWS + r, 1), :] = steps_ref[
                pl.ds(plan[ORDER + slot_of(member) * LOCAL + r], 1), :
            ]
    out[:, 2 * CHANNELS :, :] = sorted_ref[...].astype(BF16).reshape(MEMBERS, DT_ROWS, SEQ)


def silu(values):
    return values / (1.0 + jnp.exp(-values))


def mix_kernel(
    plan_ref, params_ref, received, taps_ref, arrange, weight, swapped,
    out, mine, theirs, taps_scratch, held, plan, params, arrived,
):
    scalars = [
        pltpu.make_async_copy(plan_ref, plan, arrived.at[0]),
        pltpu.make_async_copy(params_ref, params, arrived.at[1]),
    ]
    fetch = pltpu.make_async_copy(swapped, held, arrived.at[2])
    for copy in (*scalars, fetch):
        copy.start()
    member = lax.axis_index("tensor")
    slot = slot_of(member)
    group = slot // 2

    halves = []
    for core in range(2):
        total = received[core].astype(F32)
        for chip in range(1, CHIPS):
            total = total + received[2 * chip + core].astype(F32)
        halves.append(total)
    lane = lax.broadcasted_iota(jnp.int32, (1, SEQ), 1)
    summed = jnp.concatenate([half.astype(BF16) for half in halves], axis=1)
    ordered = jnp.dot(summed, arrange[...], preferred_element_type=F32)
    zx = ordered[: 2 * CHANNELS, :SEQ]
    bc = ordered[: 2 * CHANNELS, SEQ:]
    steps_raw = ordered[2 * CHANNELS :, :SEQ]

    def columns_of(chunks):
        filler = jnp.zeros((128 - 4 * len(chunks), 128), F32)
        return jnp.concatenate(chunks + [filler], axis=0).T

    state_taps = columns_of(
        [
            taps_ref[:, pl.ds(pl.multiple_of(base + group * STATE, 128), 128)]
            for base in (INNER, INNER + WIDTH_BC)
        ]
    )

    def conv(values, taps):
        total = taps[:, 3:4] * values
        for tap in range(3):
            shift = 3 - tap
            moved = jnp.where(lane >= shift, pltpu.roll(values, shift, 1), 0.0)
            total = total + taps[:, tap : tap + 1] * moved
        return silu(total).astype(BF16)

    b_values = conv(bc[:CHANNELS], state_taps[:, :4])
    c_values = conv(bc[CHANNELS:], state_taps[:, 4:8])
    scores = lax.dot_general(
        b_values.astype(F32).T.astype(BF16), c_values, (((1,), (0,)), ((), ())),
        preferred_element_type=F32,
    )
    gate = silu(zx[:CHANNELS])

    for copy in scalars:
        copy.wait()
    heads = [plan[ORDER + slot * LOCAL + r] for r in range(LOCAL)]
    taps_scratch[...] = columns_of(
        [taps_ref[:, pl.ds(pl.multiple_of((head // 4) * 128, 128), 128)] for head in heads]
    )
    x_taps = jnp.concatenate(
        [
            taps_scratch[pl.ds(pl.multiple_of((heads[r] % 4) * HEAD_DIM, HEAD_DIM), HEAD_DIM), :][
                :, 4 * r : 4 * r + 4
            ]
            for r in range(LOCAL)
        ],
        axis=0,
    )
    x_values = conv(zx[CHANNELS:], x_taps)

    row = lax.broadcasted_iota(jnp.int32, (2 * LOCAL, SEQ), 0)

    def per_head(number):
        values = jnp.zeros((2 * LOCAL, SEQ), F32)
        for r in range(LOCAL):
            values = jnp.where(row == r, params[number, heads[r]], values)
        return values

    raw = steps_raw[: 2 * LOCAL] + per_head(0)
    steps = jnp.maximum(raw, 0.0) + jnp.log1p(jnp.exp(-jnp.abs(raw)))
    rates = -steps * jnp.exp(per_head(1))
    high = rates.astype(BF16)
    rest = rates - high.astype(F32)
    middle = rest.astype(BF16)
    low = (rest - middle.astype(F32)).astype(BF16)
    source = lax.broadcasted_iota(jnp.int32, (SEQ, SEQ), 0)
    target = lax.broadcasted_iota(jnp.int32, (SEQ, SEQ), 1)
    causal = source <= target
    until = jnp.where(causal, 1.0, 0.0).astype(BF16)
    parts = jnp.dot(jnp.concatenate([high, middle, low, low], axis=0), until, preferred_element_type=F32)
    running = parts[:8] + parts[8:16] + parts[16:24]
    columns = jnp.concatenate(
        [running[:LOCAL], steps[:LOCAL], jnp.zeros((128 - 2 * LOCAL, SEQ), F32)], axis=0
    ).T

    mixed = []
    for r in range(LOCAL):
        spread = running[r : r + 1] - columns[:, r : r + 1]
        decay = jnp.exp(jnp.where(causal, spread, -1e30))
        weights = (decay * scores * columns[:, LOCAL + r : LOCAL + r + 1]).astype(BF16)
        x_head = x_values[r * HEAD_DIM : (r + 1) * HEAD_DIM]
        y_head = jnp.dot(x_head, weights, preferred_element_type=F32)
        mixed.append(y_head + params[2, heads[r]] * x_head.astype(F32))
    gated = jnp.concatenate(mixed, axis=0) * gate
    result = gated.T.astype(BF16)
    for index in range(CHIPS):
        out[index] = result
    begins = [
        plan[ORDER + (2 * row + member % 2) * PER_GROUP + offset] * HEAD_DIM
        for row in range(4)
        for offset in range(PER_GROUP)
    ]

    def sort_rows(source, sink):
        for place, begin in enumerate(begins):
            sink[place * HEAD_DIM : (place + 1) * HEAD_DIM, :] = source[
                pl.ds(pl.multiple_of(begin, HEAD_DIM), HEAD_DIM), :
            ]

    sort_rows(weight, mine)
    fetch.wait()
    sort_rows(held, theirs)


def finish_kernel(gathered, own, peer, out):
    core = lax.axis_index("tensor") % 2
    normed = []
    for row in range(4):
        values = jnp.concatenate([gathered[2 * row], gathered[2 * row + 1]], axis=1).astype(F32)
        mean_square = jnp.sum(values * values, axis=1, keepdims=True) / (PER_GROUP * HEAD_DIM)
        normed.append((values * lax.rsqrt(mean_square + epsilon)).astype(BF16))
    normed = jnp.concatenate(normed, axis=1)
    for ref, place in ((own, core), (peer, 1 - core)):
        product = jnp.dot(normed, ref[...], preferred_element_type=F32)
        out[:, :, pl.ds(pl.multiple_of(place * ROWS, ROWS), ROWS)] = product.astype(BF16).reshape(
            MEMBERS, SEQ // MEMBERS, ROWS
        )


def combine_kernel(received, out):
    for chip in range(CHIPS):
        total = received[2 * chip].astype(F32) + received[2 * chip + 1].astype(F32)
        out[:, 2 * chip * ROWS : (2 * chip + 2) * ROWS] = total.astype(BF16)


SMEM = pl.BlockSpec(memory_space=pltpu.SMEM)
VMEM = pl.BlockSpec(memory_space=pltpu.VMEM)
ANY = pl.BlockSpec(memory_space=pl.ANY)


def shards(hidden, in_weight, out_weight, conv_weight, head_params, packing, head_group):
    own = in_weight.T
    peer = lax.ppermute(own, "tensor", CORE_SWAP)
    per_chip = hidden.reshape(SEQ // MEMBERS, CHIPS, 2 * ROWS).transpose(1, 0, 2)
    acts = lax.all_to_all(
        per_chip, "tensor", split_axis=0, concat_axis=0, tiled=True, axis_index_groups=CHIP_GROUPS
    ).reshape(HALF, 2 * ROWS)

    arrange = pl.pallas_call(
        arrange_kernel,
        out_shape=jax.ShapeDtypeStruct((2 * SEQ, 2 * SEQ), BF16),
        out_specs=VMEM,
        compiler_params=pltpu.CompilerParams(vmem_limit_bytes=2 * 1024 * 1024),
        cost_estimate=pl.CostEstimate(flops=12 * 10**9, bytes_accessed=4 * 10**6, transcendentals=0),
        name="arrange",
    )()
    swapped = lax.ppermute(out_weight, "tensor", CORE_SWAP)

    partial, plan = pl.pallas_call(
        project_kernel,
        out_shape=(
            jax.ShapeDtypeStruct((MEMBERS, PACKED, SEQ), BF16),
            jax.ShapeDtypeStruct((80,), jnp.int32),
        ),
        in_specs=[ANY, ANY, VMEM, VMEM, ANY, ANY],
        out_specs=(VMEM, SMEM),
        scratch_shapes=[
            pltpu.VMEM((HEADS, SEQ), F32),
            pltpu.VMEM((MEMBERS * DT_ROWS, SEQ), F32),
            pltpu.VMEM((COLS, ROWS), BF16),
            pltpu.SMEM((5,), jnp.int32),
            pltpu.SMEM((HEADS,), jnp.int32),
            pltpu.SemaphoreType.DMA((2 + len(STREAMS),)),
        ],
        compiler_params=pltpu.CompilerParams(vmem_limit_bytes=16 * 1024 * 1024),
        name="project",
    )(packing, head_group, acts, own, peer, arrange)
    partial, swapped = lax.optimization_barrier((partial, swapped))
    received = lax.all_to_all(partial, "tensor", split_axis=0, concat_axis=0, tiled=True)

    gated, mine, theirs = pl.pallas_call(
        mix_kernel,
        out_shape=(
            jax.ShapeDtypeStruct((CHIPS, SEQ, CHANNELS), BF16),
            jax.ShapeDtypeStruct((INNER // 2, ROWS), BF16),
            jax.ShapeDtypeStruct((INNER // 2, ROWS), BF16),
        ),
        in_specs=[ANY, ANY, VMEM, VMEM, VMEM, VMEM, ANY],
        out_specs=(VMEM, VMEM, VMEM),
        scratch_shapes=[
            pltpu.VMEM((128, 128), F32),
            pltpu.VMEM((INNER, ROWS), BF16),
            pltpu.SMEM((80,), jnp.int32),
            pltpu.SMEM((3, HEADS), F32),
            pltpu.SemaphoreType.DMA((3,)),
        ],
        compiler_params=pltpu.CompilerParams(vmem_limit_bytes=8 * 1024 * 1024),
        name="mix",
    )(plan, head_params, received, conv_weight, arrange, out_weight, swapped)
    gathered = lax.all_to_all(
        gated, "tensor", split_axis=0, concat_axis=0, tiled=True, axis_index_groups=CHIP_GROUPS
    )

    share = pl.pallas_call(
        finish_kernel,
        out_shape=jax.ShapeDtypeStruct((MEMBERS, SEQ // MEMBERS, 2 * ROWS), BF16),
        in_specs=[VMEM, VMEM, VMEM],
        out_specs=VMEM,
        compiler_params=pltpu.CompilerParams(vmem_limit_bytes=8 * 1024 * 1024),
        name="finish",
    )(gathered, mine, theirs)
    pieces = lax.all_to_all(share, "tensor", split_axis=0, concat_axis=0, tiled=True)
    return pl.pallas_call(
        combine_kernel,
        out_shape=jax.ShapeDtypeStruct((SEQ // MEMBERS, D), BF16),
        in_specs=[VMEM],
        out_specs=VMEM,
        compiler_params=pltpu.CompilerParams(vmem_limit_bytes=4 * 1024 * 1024),
        name="combine",
    )(pieces)


def solution(mesh):
    in_specs = (P(("dp", "tensor"), None), P("tensor", None), P(None, "tensor"), P(), P(), P(), P())
    out_specs = P(("dp", "tensor"), None)
    return jax.shard_map(shards, mesh=mesh, in_specs=in_specs, out_specs=out_specs, check_vma=False)
```
